32 devices in a mesh: narrow: 4 (over x, core), wide: 8 (over z, y).
Axes of the slice: x: 2, y: 2, z: 4, core: 2. Of those that a mesh axis runs over, the one named last changes fastest.
Arguments:
- start_block: bfloat16 [4, 8, 32, 3584], P('narrow', 'wide'), may hold values from -360 to 360
- weights: bfloat16 [4, 8, 28, 12, 128, 128], P('narrow', 'wide'), may hold values from 0.049804688 to 1
- pattern: int32 [4, 8, 28, 12], P('narrow', 'wide'), may hold values from 0 to 33, as said below
Outputs:
- filtered_basis: float32 [4, 8, 32, 3584], P('narrow', 'wide')
The draws below stay inside these ranges and needn't reach their ends.
Inputs may be any that keep to these rules, and one draw needn't show every extreme that they name: `pattern`: slot 0 of each row block names the block itself; slots below 9, and every slot of blocks from 24 on, name blocks of the own tile; the other slots of a rim block name block value - 28 of the facing neighbour's rim that faces it.
All inputs are finite; a program needn't handle non-finite values.
Results may differ from the reference program's by a relative error of at most 0.0031.
Values may be sent and summed in bfloat16 or wider, within the bound.
No kernel may reach another device: no remote copies, remote signals or barrier semaphores. Data moves between devices by JAX's collectives and lax.ppermute only.
A program may use at most 64 MiB of HBM per device.

```python
import math
import jax
import jax.numpy as jnp
from jax import lax

NVEC = 32
BS = 128
K = 12
K_IN = 9
RIM = 6
BLK = 28
MAPR = 4
MAPC = 8
TILE_ROWS = 3584
NDOCS = 114688


def draw_start_block(key, part):
    key_base, key_rows, key_cols = jax.random.split(key, 3)
    shape = (MAPR, MAPC, NVEC, TILE_ROWS)
    tile_count = MAPR * MAPC
    position = jnp.arange(tile_count, dtype=jnp.float32).reshape(MAPR, MAPC, 1, 1)
    rising = 1.0 + 2.0 * position / max(tile_count - 1, 1)
    row_scale = jnp.exp(jax.random.uniform(key_rows, (MAPR, MAPC, 1, TILE_ROWS)) * math.log(10.0))
    col_scale = jnp.exp(jax.random.uniform(key_cols, (1, 1, NVEC, 1)) * math.log(10.0))
    base = jnp.clip(jax.random.normal(key_base, shape), -4.0, 4.0)
    return (0.3 * base * row_scale * col_scale * rising).astype(jnp.bfloat16)


def draw_pattern(key, part):
    key_inner, key_outer = jax.random.split(key, 2)
    inward = jax.random.randint(key_inner, (MAPR, MAPC, BLK, K), 0, BLK)
    outward = BLK + jax.random.randint(key_outer, (MAPR, MAPC, BLK, K), 0, RIM)
    block_ids = jnp.arange(BLK, dtype=jnp.int32).reshape(1, 1, BLK, 1)
    slot_ids = jnp.arange(K, dtype=jnp.int32).reshape(1, 1, 1, K)
    chosen = jnp.where((slot_ids >= K_IN) & (block_ids < 4 * RIM), outward, inward)
    chosen = jnp.where(slot_ids == 0, block_ids, chosen)
    return chosen.astype(jnp.int32)


def steps_of(rng, dims, cuts, low, largest):
    def one(axis_at, blocks):
        heights = jax.random.uniform(jax.random.fold_in(jax.random.fold_in(rng, 6), axis_at), (blocks,), jnp.float32, low / len(cuts), largest / len(cuts))
        return jnp.repeat(jnp.exp(heights), dims[axis_at] // blocks).reshape((-1,) + (1,) * (len(dims) - axis_at - 1))

    gain = one(*cuts[0])
    for cut in cuts[1:]:
        gain = gain * one(*cut)
    return gain


def setup_inputs(seed: int = 0) -> dict:
    key_of = jax.random.split(jax.random.key(seed), 4)
    start_block = draw_start_block(jax.random.fold_in(key_of[3], 71), 0)
    weights = jnp.clip(jnp.exp(math.log(1.0) - 2.9996462 * jax.random.uniform(key_of[1], (MAPR, MAPC, BLK, K, BS, BS), jnp.float32) ** steps_of(key_of[1], (MAPR, MAPC, BLK, K, BS, BS), ((0, 4), (1, 8)), -0.2, 0.2)), 0.049804688, 1.0).astype(jnp.bfloat16)
    pattern = draw_pattern(jax.random.fold_in(key_of[3], 71), 0)
    return {"start_block": start_block, "weights": weights, "pattern": pattern}


lower_edge = 0.3
center = (2.0 + lower_edge) / 2.0
half_width = (2.0 - lower_edge) / 2.0
highest = lax.Precision.HIGHEST
opposite_rim = (1, 0, 3, 2)

def shifted(array_in, axis_index, step_by):
    length = array_in.shape[axis_index]
    zero_rim = jnp.zeros_like(lax.slice_in_dim(array_in, 0, 1, axis=axis_index))
    if step_by > 0:
        return jnp.concatenate([zero_rim, lax.slice_in_dim(array_in, 0, length - 1, axis=axis_index)], axis=axis_index)
    return jnp.concatenate([lax.slice_in_dim(array_in, 1, length, axis=axis_index), zero_rim], axis=axis_index)

def rim_part(array_in, rim_index):
    return array_in[:, :, :, rim_index * RIM:(rim_index + 1) * RIM]

def tile_product(tile_inputs):
    weight_block, extended_values, target, values = tile_inputs
    weight_wide = weight_block.astype(jnp.float32)
    gathered = jnp.take(extended_values, target, axis=1).astype(jnp.float32)
    forward = jnp.einsum('bsrc,nbsc->nbr', weight_wide, gathered)
    transposed = jnp.einsum('bsrc,nbr->bsnc', weight_wide, values.astype(jnp.float32))
    selector = (target[:, :, None] == jnp.arange(BLK + 4 * RIM, dtype=jnp.int32)[None, None, :]).astype(jnp.float32)
    grouped = jnp.einsum('bse,bsnc->nec', selector, transposed, precision=highest)
    return (forward, grouped)

def affinity(values, weights, target):
    segments = [shifted(rim_part(values, opposite_rim[direction]), direction // 2, 1 - 2 * (direction % 2)) for direction in range(4)]
    extended_values = jnp.concatenate([values] + segments, axis=3)
    tile_count = MAPR * MAPC

    def flatten(array_in):
        return array_in.reshape((tile_count,) + array_in.shape[2:])
    forward, grouped = lax.map(tile_product, (flatten(weights), flatten(extended_values), flatten(target), flatten(values)))
    forward = forward.reshape((MAPR, MAPC) + forward.shape[1:])
    grouped = grouped.reshape((MAPR, MAPC) + grouped.shape[1:])
    own_part = grouped[:, :, :, :BLK]
    outgoing = lax.optimization_barrier(grouped[:, :, :, BLK:].astype(jnp.bfloat16)).astype(jnp.float32)
    rim_added = [shifted(rim_part(outgoing, opposite_rim[direction]), direction // 2, 1 - 2 * (direction % 2)) for direction in range(4)]
    interior = jnp.zeros((MAPR, MAPC, values.shape[2], BLK - 4 * RIM, BS), jnp.float32)
    back_terms = own_part + jnp.concatenate(rim_added + [interior], axis=3)
    return 0.5 * (forward + back_terms)

def reference(start_block, weights, pattern):
    block_ids = jnp.arange(BLK, dtype=jnp.int32).reshape(1, 1, BLK, 1)
    facing = jnp.minimum(block_ids // RIM, 3)
    target = jnp.where(pattern < BLK, pattern, BLK + facing * RIM + (pattern - BLK)).astype(jnp.int32)
    ones_block = jnp.ones((MAPR, MAPC, 1, BLK, BS), jnp.bfloat16)
    degree = affinity(ones_block, weights, target)
    inv_root = 1.0 / jnp.sqrt(degree)

    def laplace(vectors):
        scaled = (inv_root * vectors).astype(jnp.bfloat16)
        return vectors - inv_root * affinity(scaled, weights, target)
    initial = start_block.reshape(MAPR, MAPC, NVEC, BLK, BS).astype(jnp.float32)
    previous = initial
    current = (laplace(initial) - center * initial) / half_width
    for repeat in range(2):
        following = 2.0 * (laplace(current) - center * current) / half_width - previous
        previous, current = (current, following)
    gram = jnp.einsum('ijnbr,ijmbr->nm', current, current, precision=highest)
    factor = jnp.linalg.cholesky(gram)
    inverse = lax.linalg.triangular_solve(factor, jnp.eye(NVEC, dtype=jnp.float32), left_side=True, lower=True)
    flattened = jnp.transpose(current, (2, 0, 1, 3, 4)).reshape(NVEC, NDOCS)
    result_basis = jnp.dot(inverse, flattened, precision=highest) * math.sqrt(NDOCS)
    return jnp.transpose(result_basis.reshape(NVEC, MAPR, MAPC, TILE_ROWS), (1, 2, 0, 3))
```

```python
import functools
import math

import jax
import jax.numpy as jnp
from jax import lax
from jax.experimental import pallas as pl
from jax.experimental.pallas import tpu as pltpu
from jax.sharding import PartitionSpec as P

RIM = 6
RIMS = 4
INNER = 9
LANES = 128
F32 = jnp.float32
BF16 = jnp.bfloat16

lower_edge = 0.3
center = (2.0 + lower_edge) / 2.0
half_width = (2.0 - lower_edge) / 2.0

ROWS_BY_ROWS = (((1,), (1,)), ((), ()))
ROWS_BY_COLS = (((1,), (0,)), ((), ()))


def mm(left, right, dims, precision=None):
    return lax.dot_general(left, right, dims, precision=precision, preferred_element_type=F32)


def beside(parts):
    return parts[0] if len(parts) == 1 else jnp.concatenate(parts, axis=1)


def slot_pairs(first, last):
    return [list(range(s, min(s + 2, last))) for s in range(first, last, 2)]


def column(b):
    return pl.ds(b * LANES, LANES)


def outgoing_ones(pattern_ref, meta_ref, w_hbm, *refs):
    pay_refs, (w_ref, sums, sems) = refs[:4], refs[4:]
    copies = []
    for r in range(RIMS):
        rows = pl.ds(r * RIM, RIM)
        copies.append(pltpu.make_async_copy(w_hbm.at[rows, INNER:], w_ref.at[rows], sems.at[r]))
        copies[-1].start()
    slots = w_ref.shape[1]
    sums[...] = jnp.zeros_like(sums)
    ones = jnp.ones((8, LANES), BF16)
    for r in range(RIMS):
        copies[r].wait()
        for b in range(r * RIM, (r + 1) * RIM):
            part = mm(ones, beside([w_ref[b, s] for s in range(slots)]), ROWS_BY_COLS)
            for s in range(slots):
                q = pattern_ref[b, INNER + s] - pattern_ref.shape[0]
                sums[r, pl.ds(q, 1)] += part[0:1, s * LANES : (s + 1) * LANES]
    for m in range(4):
        pay_refs[m][...] = sums[meta_ref[m]].astype(BF16).astype(F32)


def local_degree(pattern_ref, meta_ref, w_ref, deg_ref, acc):
    blocks, slots = w_ref.shape[:2]
    acc[...] = jnp.zeros_like(acc)
    ones = jnp.ones((8, LANES), BF16)
    for b in range(blocks):
        own = INNER if b < RIMS * RIM else slots
        for group in slot_pairs(0, own):
            part = mm(ones, beside([w_ref[b, s] for s in group]), ROWS_BY_COLS)
            for i, s in enumerate(group):
                acc[pl.ds(pattern_ref[b, s], 1)] += part[0:1, i * LANES : (i + 1) * LANES]
        rows = w_ref[b, 0].astype(F32)
        for s in range(1, own):
            rows = rows + w_ref[b, s].astype(F32)
        if own < slots:
            outer = w_ref[b, own].astype(F32)
            for s in range(own + 1, slots):
                outer = outer + w_ref[b, s].astype(F32)
            rows = rows + meta_ref[8 + b // RIM].astype(F32) * outer
        high = rows.astype(BF16)
        rest = rows - high.astype(F32)
        mid = rest.astype(BF16)
        low = (rest - mid.astype(F32)).astype(BF16)
        wide_ones = jnp.ones((8, 3 * LANES), BF16)
        total = mm(wide_ones, beside([high, mid, low]), ROWS_BY_ROWS)
        deg_ref[pl.ds(b, 1)] = total[0:1]
    deg_ref[...] = deg_ref[...] + acc[...]


def send_out(u_ref, w_ref, pattern_ref, meta_ref, terms, pay_refs):
    blocks, slots = w_ref.shape[:2]
    terms[...] = jnp.zeros_like(terms)
    for b in range(RIMS * RIM):
        part = mm(u_ref[b], beside([w_ref[b, s] for s in range(INNER, slots)]), ROWS_BY_COLS)
        base = (b // RIM) * RIM - blocks
        for s in range(INNER, slots):
            i = s - INNER
            terms[base + pattern_ref[b, s]] += part[:, i * LANES : (i + 1) * LANES]
    for m in range(4):
        first = meta_ref[m] * RIM
        pay_refs[m][0:RIM] = u_ref[pl.ds(first, RIM)]
        pay_refs[m][RIM:] = terms[pl.ds(first, RIM)].astype(BF16)


def first_scaled(pattern_ref, meta_ref, w_ref, deg_ref, x_ref, *refs):
    in_refs, (inv_ref, u_ref), pay_refs, (rims, terms) = refs[:4], refs[4:6], refs[6:10], refs[10:]
    blocks = w_ref.shape[0]
    for m in range(4):
        rims[meta_ref[m]] = in_refs[m][...] * meta_ref[4 + m].astype(F32)
    for b in range(blocks):
        degree = deg_ref[b : b + 1]
        if b < RIMS * RIM:
            degree = degree + rims[b // RIM, b % RIM : b % RIM + 1]
        inv = 1.0 / jnp.sqrt(0.5 * degree)
        inv_ref[b : b + 1] = inv
        u_ref[b] = (inv * x_ref[:, column(b)].astype(F32)).astype(BF16)
    send_out(u_ref, w_ref, pattern_ref, meta_ref, terms, pay_refs)


def own_terms(pattern_ref, meta_ref, w_ref, u_ref, acc_ref, forward):
    blocks, slots = w_ref.shape[:2]
    acc_ref[...] = jnp.zeros_like(acc_ref)
    for b in range(blocks):
        total = None
        own = INNER if b < RIMS * RIM else slots
        for group in slot_pairs(0, own):
            w = beside([w_ref[b, s] for s in group])
            part = mm(u_ref[b], w, ROWS_BY_COLS)
            for i, s in enumerate(group):
                acc_ref[pattern_ref[b, s]] += part[:, i * LANES : (i + 1) * LANES]
            ahead = mm(beside([u_ref[pattern_ref[b, s]] for s in group]), w, ROWS_BY_ROWS)
            total = ahead if total is None else total + ahead
        forward[b] = total
    acc_ref[...] += forward[...]


def combine(step, pattern_ref, meta_ref, w_ref, inv_ref, acc_ref, in_refs, y_ref, before_ref, next_ref, ext, u_ref):
    blocks, slots = w_ref.shape[:2]
    for m in range(4):
        live = meta_ref[4 + m].astype(BF16)
        first = meta_ref[m] * 2 * RIM
        ext[pl.ds(first, 2 * RIM)] = in_refs[m][...] * live
    for b in range(blocks):
        total = acc_ref[b]
        if b < RIMS * RIM:
            base = (b // RIM) * 2 * RIM
            ahead = beside([ext[base + pattern_ref[b, s] - blocks] for s in range(INNER, slots)])
            total = total + mm(ahead, beside([w_ref[b, s] for s in range(INNER, slots)]), ROWS_BY_ROWS)
            total = total + ext[base + RIM + b % RIM].astype(F32)
        inv = inv_ref[b : b + 1]
        y = y_ref[:, column(b)].astype(F32)
        lap = y - inv * (0.5 * total)
        new = (lap - center * y) / half_width
        if step > 0:
            new = 2.0 * new - before_ref[:, column(b)].astype(F32)
        next_ref[:, column(b)] = new
        if u_ref is not None:
            u_ref[b] = (inv * new).astype(BF16)


def advance(step, pattern_ref, meta_ref, w_ref, inv_ref, acc_ref, *refs):
    in_refs, (y_ref, before_ref, next_ref, u_ref) = refs[:4], refs[4:8]
    pay_refs, (ext, terms) = refs[8:12], refs[12:]
    combine(step, pattern_ref, meta_ref, w_ref, inv_ref, acc_ref, in_refs, y_ref, before_ref, next_ref, ext, u_ref)
    send_out(u_ref, w_ref, pattern_ref, meta_ref, terms, pay_refs)


def finish(pattern_ref, meta_ref, w_ref, inv_ref, acc_ref, *refs):
    in_refs, (y_ref, before_ref, next_ref, gram_ref, ext) = refs[:4], refs[4:]
    combine(2, pattern_ref, meta_ref, w_ref, inv_ref, acc_ref, in_refs, y_ref, before_ref, next_ref, ext, None)
    y = next_ref[...]
    gram = mm(y, y, ROWS_BY_ROWS, lax.Precision.HIGHEST)
    packed = beside([gram[8 * i : 8 * i + 8] for i in range(gram.shape[0] // 8)])
    gram_ref[...] = jnp.broadcast_to(packed[None], gram_ref.shape)


def orthonormal(scale, grams_ref, y_ref, out_ref):
    packed = jnp.sum(grams_ref[...], axis=0)
    n = y_ref.shape[0]
    gram = jnp.concatenate([packed[:, n * i : n * (i + 1)] for i in range(n // 8)], axis=0)
    row_id = lax.broadcasted_iota(jnp.int32, (n, n), 0)
    col_id = lax.broadcasted_iota(jnp.int32, (n, n), 1)
    eye = (row_id == col_id).astype(F32)
    both = jnp.concatenate([gram, eye], axis=1)
    rows = lax.broadcasted_iota(jnp.int32, (n, 2 * n), 0)
    roots = jnp.zeros((n, 1), F32)
    row_of = lax.broadcasted_iota(jnp.int32, (n, 1), 0)
    for k in range(n):
        pivot_row = both[k : k + 1]
        pivot = both[k : k + 1, k : k + 1]
        roots = jnp.where(row_of == k, pivot, roots)
        if k < n - 1:
            factor = jnp.where(row_of > k, both[:, k : k + 1] / pivot, 0.0)
            both = both - factor * pivot_row
    inverse = both[:, n:] * (scale / jnp.sqrt(roots))
    out_ref[...] = mm(inverse, y_ref[...], ROWS_BY_COLS, lax.Precision.HIGHEST)


def in_vmem(x):
    return pltpu.with_memory_space_constraint(x, pltpu.VMEM)


def kernel_call(body, name, ins, outs, scratch=(), flops=0, moved=0):
    specs, args = [], []
    for kind, x in ins:
        if kind == "hbm":
            specs.append(pl.BlockSpec(memory_space=pl.ANY))
        elif kind == "smem":
            specs.append(pl.BlockSpec(memory_space=pltpu.SMEM))
        else:
            specs.append(pl.BlockSpec(memory_space=pltpu.VMEM))
            if kind == "held":
                x = in_vmem(x)
        args.append(x)
    return pl.pallas_call(
        body,
        name=name,
        out_shape=[jax.ShapeDtypeStruct(s, d) for s, d in outs],
        in_specs=specs,
        out_specs=[pl.BlockSpec(memory_space=pltpu.VMEM)] * len(outs),
        scratch_shapes=list(scratch),
        compiler_params=pltpu.CompilerParams(vmem_limit_bytes=16 << 20),
        cost_estimate=pl.CostEstimate(flops=flops, bytes_accessed=moved, transcendentals=0),
    )(*args)


def matchings(axis):
    peers = lax.axis_size(axis)
    pairs = []
    for first in (0, 1):
        swaps = []
        for i in range(first, peers, 2):
            j = (i + 1) % peers
            swaps += [(i, j), (j, i)]
        pairs.append(swaps)
    return pairs


def exchange(payloads):
    got = [None] * 4
    for a, axis in ((1, "wide"), (0, "narrow")):
        pairs = matchings(axis)
        for m in (1, 0):
            got[2 * a + m] = lax.ppermute(payloads[2 * a + m], axis, pairs[m])
    return got


def placement():
    sends, live, by_rim = [], [], []
    for a, axis in enumerate(("narrow", "wide")):
        place = lax.axis_index(axis)
        last = lax.axis_size(axis) - 1
        for m in (0, 1):
            after = (place + m) % 2 == 0
            sends.append(2 * a + after.astype(jnp.int32))
            live.append(jnp.where(after, place < last, place > 0).astype(jnp.int32))
        by_rim += [(place > 0).astype(jnp.int32), (place < last).astype(jnp.int32)]
    return jnp.stack(sends + live + by_rim)


def body(start_block, weights, pattern):
    x = start_block[0, 0]
    w = weights[0, 0]
    slots_of = pattern[0, 0]
    meta = placement()
    vecs, docs = x.shape
    blocks, slots = w.shape[:2]
    rows = RIMS * RIM
    ids = [("smem", slots_of), ("smem", meta)]
    tile = ((blocks, vecs, LANES), F32)
    scaled = ((blocks, vecs, LANES), BF16)
    full = ((vecs, docs), F32)
    payload = [((2 * RIM, vecs, LANES), BF16)] * 4
    held = ids + [("held", w)]
    per_block = 2 * LANES * LANES

    pays = kernel_call(
        outgoing_ones, "outgoing_ones", ids + [("hbm", w)], [((8, LANES), F32)] * 4,
        [pltpu.VMEM((rows, slots - INNER, LANES, LANES), BF16), pltpu.VMEM((RIMS, 8, LANES), F32),
         pltpu.SemaphoreType.DMA((RIMS,))],
        flops=rows * 3 * per_block * 32, moved=1 << 20,
    )
    (degree,) = kernel_call(
        local_degree, "local_degree", held, [((blocks, LANES), F32)], [pltpu.VMEM((blocks, LANES), F32)],
        flops=blocks * slots * per_block * 32, moved=8 << 20,
    )
    got = exchange(pays)
    inv, u, *pays = kernel_call(
        first_scaled, "first_scaled",
        held + [("vmem", degree), ("vmem", x)] + [("vmem", g) for g in got],
        [((blocks, LANES), F32), scaled] + payload,
        [pltpu.VMEM((RIMS, 8, LANES), F32), pltpu.VMEM((rows, vecs, LANES), F32)],
        flops=rows * 3 * per_block * 32, moved=1 << 20,
    )
    before, y = x, x
    for step in range(3):
        (acc,) = kernel_call(
            own_terms, "own_terms", held + [("vmem", u)], [tile],
            [pltpu.VMEM(*tile)],
            flops=2 * blocks * slots * per_block * vecs, moved=8 << 20,
        )
        got = exchange(pays)
        common = held + [("vmem", inv), ("vmem", acc)] + [("vmem", g) for g in got] + [("vmem", y), ("vmem", before)]
        ext = pltpu.VMEM((2 * rows, vecs, LANES), BF16)
        if step < 2:
            new, u, *pays = kernel_call(
                functools.partial(advance, step), "advance", common, [full, scaled] + payload,
                [ext, pltpu.VMEM((rows, vecs, LANES), F32)],
                flops=2 * rows * 3 * per_block * 32, moved=1 << 20,
            )
        else:
            peers = lax.axis_size("narrow") * lax.axis_size("wide")
            new, grams = kernel_call(
                finish, "finish", common, [full, ((peers, 8, LANES), F32)], [ext],
                flops=rows * 3 * per_block * 32, moved=1 << 20,
            )
        before, y = y, new
    grams = lax.all_to_all(grams, ("narrow", "wide"), 0, 0)
    (out,) = kernel_call(
        functools.partial(orthonormal, math.sqrt(peers * docs)), "orthonormal",
        [("vmem", grams), ("vmem", y)], [full],
    )
    return out[None, None]


def solution(mesh):
    placed = (
        P("narrow", "wide", None, None),
        P("narrow", "wide", None, None, None, None),
        P("narrow", "wide", None, None),
    )
    return jax.shard_map(
        body, mesh=mesh, in_specs=placed, out_specs=P("narrow", "wide", None, None), check_vma=False
    )
```

```python
import functools
import math

import jax
import jax.numpy as jnp
from jax import lax
from jax.experimental import pallas as pl
from jax.experimental.pallas import tpu as pltpu
from jax.sharding import PartitionSpec as P

RIM = 6
RIMS = 4
INNER = 9
LANES = 128
F32 = jnp.float32
BF16 = jnp.bfloat16

lower_edge = 0.3
center = (2.0 + lower_edge) / 2.0
half_width = (2.0 - lower_edge) / 2.0

ROWS_BY_ROWS = (((1,), (1,)), ((), ()))
ROWS_BY_COLS = (((1,), (0,)), ((), ()))


def mm(left, right, dims, precision=None):
    return lax.dot_general(left, right, dims, precision=precision, preferred_element_type=F32)


def beside(parts):
    return parts[0] if len(parts) == 1 else jnp.concatenate(parts, axis=1)


def over(parts):
    return parts[0] if len(parts) == 1 else jnp.concatenate(parts, axis=0)


def slot_pairs(first, last):
    return [list(range(s, min(s + 2, last))) for s in range(first, last, 2)]


def column(b):
    return pl.ds(b * LANES, LANES)


ORDER = (3, 1, 2, 0)


def outgoing_ones(meta_ref, pattern_hbm, w_hbm, *refs):
    pay_refs, (w_ref, pattern_ref, sums, sems) = refs[:4], refs[4:]
    copies = []
    for r in range(RIMS):
        rows = pl.ds(r * RIM, RIM)
        copies.append(pltpu.make_async_copy(w_hbm.at[rows, INNER:], w_ref.at[rows], sems.at[r]))
        copies[-1].start()
    copies.append(pltpu.make_async_copy(pattern_hbm, pattern_ref, sems.at[RIMS]))
    copies[-1].start()
    copies[-1].wait()
    slots = w_ref.shape[1]
    sums[...] = jnp.zeros_like(sums)
    ones = jnp.ones((8, LANES), BF16)
    for r in range(RIMS):
        copies[r].wait()
        for b in range(r * RIM, (r + 1) * RIM):
            part = mm(ones, beside([w_ref[b, s] for s in range(slots)]), ROWS_BY_COLS)
            for s in range(slots):
                q = pattern_ref[INNER + s, 0, b] - pattern_ref.shape[2]
                sums[r, pl.ds(q, 1)] += part[0:1, s * LANES : (s + 1) * LANES]
    for m in range(4):
        pay_refs[m][...] = sums[meta_ref[m]].astype(BF16).astype(F32)


def local_degree(pattern_ref, meta_ref, w_ref, deg_ref, acc):
    blocks, slots = w_ref.shape[:2]
    acc[...] = jnp.zeros_like(acc)
    ones = jnp.ones((8, LANES), BF16)
    wide_ones = jnp.ones((8, 3 * LANES), BF16)
    for b in range(blocks):
        own = INNER if b < RIMS * RIM else slots
        for group in slot_pairs(0, own):
            part = mm(ones, beside([w_ref[b, s] for s in group]), ROWS_BY_COLS)
            for i, s in enumerate(group):
                acc[pattern_ref[s, 0, b]] += part[:, i * LANES : (i + 1) * LANES]
        rows = w_ref[b, 0].astype(F32)
        for s in range(1, own):
            rows = rows + w_ref[b, s].astype(F32)
        if own < slots:
            outer = w_ref[b, own].astype(F32)
            for s in range(own + 1, slots):
                outer = outer + w_ref[b, s].astype(F32)
            rows = rows + meta_ref[8 + b // RIM].astype(F32) * outer
        high = rows.astype(BF16)
        rest = rows - high.astype(F32)
        mid = rest.astype(BF16)
        low = (rest - mid.astype(F32)).astype(BF16)
        total = mm(wide_ones, beside([high, mid, low]), ROWS_BY_ROWS)
        deg_ref[b : b + 1] = total[0:1]
    for b in range(blocks):
        deg_ref[b : b + 1] += acc[b, 0:1]


def send_out(u_ref, w_ref, pattern_ref, meta_ref, terms, pay_refs):
    blocks, slots = w_ref.shape[:2]
    terms[...] = jnp.zeros_like(terms)
    for b in range(RIMS * RIM):
        part = mm(u_ref[b], beside([w_ref[b, s] for s in range(INNER, slots)]), ROWS_BY_COLS)
        base = (b // RIM) * RIM - blocks
        for s in range(INNER, slots):
            i = s - INNER
            terms[base + pattern_ref[s, 0, b]] += part[:, i * LANES : (i + 1) * LANES]
    for m in range(4):
        first = meta_ref[m] * RIM
        pay_refs[m][0:RIM] = u_ref[pl.ds(first, RIM)]
        pay_refs[m][RIM:] = terms[pl.ds(first, RIM)].astype(BF16)


def first_scaled(pattern_ref, meta_ref, w_ref, deg_ref, x_ref, *refs):
    in_refs, (inv_ref, u_ref), pay_refs, (rims, terms) = refs[:4], refs[4:6], refs[6:10], refs[10:]
    blocks = w_ref.shape[0]
    for m in range(4):
        rims[meta_ref[m]] = in_refs[m][...] * meta_ref[4 + m].astype(F32)
    for b in range(blocks):
        degree = deg_ref[b : b + 1]
        if b < RIMS * RIM:
            degree = degree + rims[b // RIM, b % RIM : b % RIM + 1]
        inv = 1.0 / jnp.sqrt(0.5 * degree)
        inv_ref[b : b + 1] = inv
        u_ref[b] = (inv * x_ref[:, column(b)].astype(F32)).astype(BF16)
    send_out(u_ref, w_ref, pattern_ref, meta_ref, terms, pay_refs)


def own_products(pattern_ref, w_ref, turned, u_ref, acc_ref):
    blocks, slots = w_ref.shape[:2]
    acc_ref[...] = jnp.zeros_like(acc_ref)
    for b in range(blocks):
        total = None
        own = INNER if b < RIMS * RIM else slots
        for group in slot_pairs(0, own):
            part = mm(u_ref[b], beside([w_ref[b, s] for s in group]), ROWS_BY_COLS)
            for i, s in enumerate(group):
                acc_ref[pattern_ref[s, 0, b]] += part[:, i * LANES : (i + 1) * LANES]
            ahead = beside([u_ref[pattern_ref[s, 0, b]] for s in group])
            ahead = mm(ahead, over([turned(b, s) for s in group]), ROWS_BY_COLS)
            total = ahead if total is None else total + ahead
        acc_ref[b] += total


def own_terms(pattern_ref, w_ref, turned_ref, u_ref, acc_ref):
    own_products(pattern_ref, w_ref, lambda b, s: turned_ref[b, s], u_ref, acc_ref)


def own_terms_turning(pattern_ref, w_ref, u_ref, acc_ref, turned_ref):
    blocks, slots = w_ref.shape[:2]

    def turned(b, s):
        block = w_ref[b, s].T
        turned_ref[b, s] = block
        return block

    own_products(pattern_ref, w_ref, turned, u_ref, acc_ref)
    for b in range(RIMS * RIM):
        for s in range(INNER, slots):
            turned(b, s)


def combine(step, pattern_ref, meta_ref, turned_ref, inv_ref, acc_ref, in_refs, y_ref, before_ref, next_ref, ext, u_ref):
    blocks, slots = turned_ref.shape[:2]
    for m in range(4):
        live = meta_ref[4 + m].astype(BF16)
        first = meta_ref[m] * 2 * RIM
        ext[pl.ds(first, 2 * RIM)] = in_refs[m][...] * live
    for b in range(blocks):
        total = acc_ref[b]
        if b < RIMS * RIM:
            base = (b // RIM) * 2 * RIM
            ahead = beside([ext[base + pattern_ref[s, 0, b] - blocks] for s in range(INNER, slots)])
            total = total + mm(ahead, over([turned_ref[b, s] for s in range(INNER, slots)]), ROWS_BY_COLS)
            total = total + ext[base + RIM + b % RIM].astype(F32)
        inv = inv_ref[b : b + 1]
        y = y_ref[:, column(b)].astype(F32)
        lap = y - inv * (0.5 * total)
        new = (lap - center * y) / half_width
        if step > 0:
            new = 2.0 * new - before_ref[:, column(b)].astype(F32)
        next_ref[:, column(b)] = new
        if u_ref is not None:
            u_ref[b] = (inv * new).astype(BF16)


def advance(step, pattern_ref, meta_ref, w_ref, turned_ref, inv_ref, acc_ref, *refs):
    in_refs, (y_ref, before_ref, next_ref, u_ref) = refs[:4], refs[4:8]
    pay_refs, (ext, terms) = refs[8:12], refs[12:]
    combine(step, pattern_ref, meta_ref, turned_ref, inv_ref, acc_ref, in_refs, y_ref, before_ref, next_ref, ext, u_ref)
    send_out(u_ref, w_ref, pattern_ref, meta_ref, terms, pay_refs)


def finish(pattern_ref, meta_ref, turned_ref, inv_ref, acc_ref, *refs):
    in_refs, (y_ref, before_ref, next_ref, gram_ref, ext) = refs[:4], refs[4:]
    combine(2, pattern_ref, meta_ref, turned_ref, inv_ref, acc_ref, in_refs, y_ref, before_ref, next_ref, ext, None)
    y = next_ref[...]
    gram = mm(y, y, ROWS_BY_ROWS, lax.Precision.HIGHEST)
    packed = beside([gram[8 * i : 8 * i + 8] for i in range(gram.shape[0] // 8)])
    gram_ref[...] = jnp.broadcast_to(packed[None], gram_ref.shape)


def inverse_factor(gram, scale):
    n = gram.shape[0]
    tall = 8
    groups = range(n // tall)
    lane = lax.broadcasted_iota(jnp.int32, (tall, LANES), 1)
    sub = lax.broadcasted_iota(jnp.int32, (tall, LANES), 0)

    def spread(values, r):
        return jnp.broadcast_to(values[r : r + 1], (tall, LANES))

    both = []
    for i in groups:
        eye = (lane[:, :n] == sub[:, :n] + tall * i).astype(F32)
        both.append(beside([gram[tall * i : tall * (i + 1)], eye, jnp.zeros((tall, LANES - 2 * n), F32)]))
    parts = []
    for q in groups:
        columns = [
            {i: jnp.broadcast_to(both[i][:, tall * q + j : tall * q + j + 1], (tall, LANES)) for i in groups if i >= q}
            for j in range(tall)
        ]
        pivots = None
        for r in range(tall):
            pivot = spread(columns[r][q], r)
            pivots = pivot if pivots is None else jnp.where(sub == r, pivot, pivots)
            inv = 1.0 / pivot
            row = spread(both[q], r) * inv
            below = dict(columns[r])
            below[q] = jnp.where(sub > r, below[q], 0.0)
            live = [i for i in groups if i > q or (i == q and r < tall - 1)]
            for j in range(r + 1, tall):
                scaled = spread(columns[j][q], r) * inv
                for i in live:
                    columns[j][i] = columns[j][i] - below[i] * scaled
            for i in live:
                both[i] = both[i] - below[i] * row
        parts.append((both[q] * (scale / jnp.sqrt(pivots)))[:, n : 2 * n])
    return over(parts)


def orthonormal(scale, grams_ref, y_ref, out_ref):
    packed = jnp.sum(grams_ref[...], axis=0)
    n = y_ref.shape[0]
    gram = over([packed[:, n * i : n * (i + 1)] for i in range(n // 8)])
    out_ref[...] = mm(inverse_factor(gram, scale), y_ref[...], ROWS_BY_COLS, lax.Precision.HIGHEST)


def in_vmem(x):
    return pltpu.with_memory_space_constraint(x, pltpu.VMEM)


def kernel_call(body, name, ins, outs, scratch=(), flops=0, moved=0):
    specs, args = [], []
    for kind, x in ins:
        if kind == "hbm":
            specs.append(pl.BlockSpec(memory_space=pl.ANY))
            x = pltpu.with_memory_space_constraint(x, pltpu.HBM)
        elif kind == "smem":
            specs.append(pl.BlockSpec(memory_space=pltpu.SMEM))
            x = pltpu.with_memory_space_constraint(x, pltpu.SMEM)
        else:
            specs.append(pl.BlockSpec(memory_space=pltpu.VMEM))
            if kind == "held":
                x = in_vmem(x)
        args.append(x)
    return pl.pallas_call(
        body,
        name=name,
        out_shape=[pltpu.VMEM(s, d) if len(s) == 4 else jax.ShapeDtypeStruct(s, d) for s, d in outs],
        in_specs=specs,
        out_specs=[pl.BlockSpec(memory_space=pltpu.VMEM)] * len(outs),
        scratch_shapes=list(scratch),
        compiler_params=pltpu.CompilerParams(vmem_limit_bytes=16 << 20),
        cost_estimate=pl.CostEstimate(flops=flops, bytes_accessed=moved, transcendentals=0),
    )(*args)


def swaps():
    tall, broad = lax.axis_size("narrow"), lax.axis_size("wide")
    found = []
    for m in (0, 1):
        pairs = []
        for w in range(broad):
            for i in range(m, tall - 1, 2):
                pairs.append(((i, w), (i + 1, w)))
        if m == 1 and tall <= 4:
            pairs += [((0, w), (tall - 1, w)) for w in range(broad)]
        elif m == 1:
            pairs += [((i, w), (i, w + 1)) for i in (0, tall - 1) for w in range(0, broad, 2)]
        found.append(pairs)
    for m in (0, 1):
        pairs = []
        for i in range(tall):
            for w in range(m, broad - 1, 2):
                pairs.append(((i, w), (i, w + 1)))
        if m == 1:
            pairs += [((i, w), (i + 1, w)) for w in (0, broad - 1) for i in range(0, tall, 2)]
        found.append(pairs)
    flat = []
    for pairs in found:
        ends = [(a[0] * broad + a[1], b[0] * broad + b[1]) for a, b in pairs]
        flat.append([p for a, b in ends for p in ((a, b), (b, a))])
    return flat


def exchange(payloads):
    pairs = swaps()
    return [lax.ppermute(payload, ("narrow", "wide"), pairs[m]) for payload, m in zip(payloads, ORDER)]


def placement():
    sends, live, by_rim = [], [], []
    for a, axis in enumerate(("narrow", "wide")):
        place = lax.axis_index(axis)
        last = lax.axis_size(axis) - 1
        for m in (0, 1):
            after = (place + m) % 2 == 0
            sends.append(2 * a + after.astype(jnp.int32))
            live.append(jnp.where(after, place < last, place > 0).astype(jnp.int32))
        by_rim += [(place > 0).astype(jnp.int32), (place < last).astype(jnp.int32)]
    return jnp.stack([sends[m] for m in ORDER] + [live[m] for m in ORDER] + by_rim)


def body(start_block, weights, pattern):
    x = start_block[0, 0]
    w = weights[0, 0]
    slots_of = jnp.transpose(pattern, (0, 3, 1, 2))[0]
    meta = placement()
    vecs, docs = x.shape
    blocks, slots = w.shape[:2]
    rows = RIMS * RIM
    ids = [("smem", slots_of), ("smem", meta)]
    tile = ((blocks, vecs, LANES), F32)
    scaled = ((blocks, vecs, LANES), BF16)
    full = ((vecs, docs), F32)
    payload = [((2 * RIM, vecs, LANES), BF16)] * 4
    per_block = 2 * LANES * LANES

    pays = kernel_call(
        outgoing_ones, "outgoing_ones", ids[1:] + [("hbm", slots_of), ("hbm", w)], [((8, LANES), F32)] * 4,
        [pltpu.VMEM((rows, slots - INNER, LANES, LANES), BF16), pltpu.SMEM(slots_of.shape, jnp.int32),
         pltpu.VMEM((RIMS, 8, LANES), F32), pltpu.SemaphoreType.DMA((RIMS + 1,))],
        flops=rows * 3 * per_block * 32, moved=1 << 20,
    )
    w, *pays = lax.optimization_barrier((w, *pays))
    held = ids + [("held", w)]
    (degree,) = kernel_call(
        local_degree, "local_degree", held, [((blocks, LANES), F32)],
        [pltpu.VMEM((blocks, 8, LANES), F32)],
        flops=blocks * slots * per_block * 32, moved=8 << 20,
    )
    got = exchange(pays)
    inv, u, *pays = kernel_call(
        first_scaled, "first_scaled",
        held + [("vmem", degree), ("vmem", x)] + [("vmem", g) for g in got],
        [((blocks, LANES), F32), scaled] + payload,
        [pltpu.VMEM((RIMS, 8, LANES), F32), pltpu.VMEM((rows, vecs, LANES), F32)],
        flops=rows * 3 * per_block * 32, moved=1 << 20,
    )
    before, y = x, x
    for step in range(3):
        cost = dict(flops=2 * blocks * slots * per_block * vecs, moved=8 << 20)
        if step == 0:
            acc, turned = kernel_call(
                own_terms_turning, "own_terms_turning", ids[:1] + [("held", w), ("vmem", u)], [tile, (w.shape, BF16)], **cost
            )
        else:
            (acc,) = kernel_call(
                own_terms, "own_terms", ids[:1] + [("held", w), ("held", turned), ("vmem", u)], [tile], **cost
            )
        got = exchange(pays)
        common = [("held", turned), ("vmem", inv), ("vmem", acc)] + [("vmem", g) for g in got]
        common += [("vmem", y), ("vmem", before)]
        ext = pltpu.VMEM((2 * rows, vecs, LANES), BF16)
        if step < 2:
            new, u, *pays = kernel_call(
                functools.partial(advance, step), "advance", held + common, [full, scaled] + payload,
                [ext, pltpu.VMEM((rows, vecs, LANES), F32)],
                flops=2 * rows * 3 * per_block * 32, moved=1 << 20,
            )
        else:
            peers = lax.axis_size("narrow") * lax.axis_size("wide")
            new, grams = kernel_call(
                finish, "finish", ids + common, [full, ((peers, 8, LANES), F32)], [ext],
                flops=rows * 3 * per_block * 32, moved=1 << 20,
            )
        before, y = y, new
    grams = lax.all_to_all(grams, ("narrow", "wide"), 0, 0)
    (out,) = kernel_call(
        functools.partial(orthonormal, math.sqrt(peers * docs)), "orthonormal",
        [("vmem", grams), ("vmem", y)], [full],
    )
    return out[None, None]


def solution(mesh):
    placed = (
        P("narrow", "wide", None, None),
        P("narrow", "wide", None, None, None, None),
        P("narrow", "wide", None, None),
    )
    return jax.shard_map(
        body, mesh=mesh, in_specs=placed, out_specs=P("narrow", "wide", None, None), check_vma=False
    )
```

```python
import functools
import math

import jax
import jax.numpy as jnp
from jax import lax
from jax.experimental import pallas as pl
from jax.experimental.pallas import tpu as pltpu
from jax.sharding import PartitionSpec as P

RIM = 6
RIMS = 4
INNER = 9
LANES = 128
F32 = jnp.float32
BF16 = jnp.bfloat16

lower_edge = 0.3
center = (2.0 + lower_edge) / 2.0
half_width = (2.0 - lower_edge) / 2.0

ROWS_BY_ROWS = (((1,), (1,)), ((), ()))
ROWS_BY_COLS = (((1,), (0,)), ((), ()))


def mm(left, right, dims, precision=None):
    return lax.dot_general(left, right, dims, precision=precision, preferred_element_type=F32)


def beside(parts):
    return parts[0] if len(parts) == 1 else jnp.concatenate(parts, axis=1)


def over(parts):
    return parts[0] if len(parts) == 1 else jnp.concatenate(parts, axis=0)


def slot_pairs(first, last):
    return [list(range(s, min(s + 2, last))) for s in range(first, last, 2)]


def column(b):
    return pl.ds(b * LANES, LANES)


ORDER = (3, 1, 2, 0)


def places(shape):
    rim_of, live_of, by_rim = [], [], []
    for a, axis in enumerate(("narrow", "wide")):
        place = lax.axis_index(axis)
        behind = (place > 0).astype(jnp.int32)
        ahead = (place < shape[a] - 1).astype(jnp.int32)
        odd = lax.rem(place, 2)
        for m in (0, 1):
            after = odd if m else 1 - odd
            rim_of.append(2 * a + after)
            live_of.append(after * ahead + (1 - after) * behind)
        by_rim += [behind, ahead]
    return [rim_of[m] for m in ORDER], [live_of[m] for m in ORDER], by_rim


def fetch(source, target, sem):
    copy = pltpu.make_async_copy(source, target, sem)
    copy.start()
    return copy


def outgoing_ones(shape, pattern_hbm, w_hbm, *refs):
    pay_refs, (pattern_ref, w_ref, sums, sems) = refs[:4], refs[4:]
    named = fetch(pattern_hbm, pattern_ref, sems.at[RIMS])
    copies = []
    for r in range(RIMS):
        rows = pl.ds(r * RIM, RIM)
        copies.append(fetch(w_hbm.at[rows, INNER:], w_ref.at[rows], sems.at[r]))
    blocks = pattern_ref.shape[2]
    slots = w_ref.shape[1]
    sums[...] = jnp.zeros_like(sums)
    ones = jnp.ones((8, LANES), BF16)
    named.wait()
    for r in range(RIMS):
        copies[r].wait()
        for b in range(r * RIM, (r + 1) * RIM):
            part = mm(ones, beside([w_ref[b, s] for s in range(slots)]), ROWS_BY_COLS)
            for s in range(slots):
                sums[r * RIM - blocks + pattern_ref[INNER + s, 0, b]] += part[:, s * LANES : (s + 1) * LANES]
    rim_of, _, _ = places(shape)
    for m in range(4):
        for q in range(RIM):
            pay_refs[m][q : q + 1] = sums[rim_of[m] * RIM + q][0:1].astype(BF16).astype(F32)


def local_degree(shape, pattern_ref, w_ref, deg_ref, acc):
    blocks, slots = w_ref.shape[:2]
    by_rim = places(shape)[2]
    ones = jnp.ones((8, LANES), BF16)
    for b in range(0, blocks, 2):
        part = mm(ones, beside([w_ref[b, 0], w_ref[b + 1, 0]]), ROWS_BY_COLS)
        acc[b] = part[:, :LANES]
        acc[b + 1] = part[:, LANES:]
    for b in range(blocks):
        own = INNER if b < RIMS * RIM else slots
        for group in slot_pairs(1, own):
            part = mm(ones, beside([w_ref[b, s] for s in group]), ROWS_BY_COLS)
            for i, s in enumerate(group):
                acc[pattern_ref[s, 0, b]] += part[:, i * LANES : (i + 1) * LANES]
        rows = w_ref[b, 0].astype(F32)
        for s in range(1, own):
            rows = rows + w_ref[b, s].astype(F32)
        if own < slots:
            outer = w_ref[b, own].astype(F32)
            for s in range(own + 1, slots):
                outer = outer + w_ref[b, s].astype(F32)
            rows = rows + by_rim[b // RIM].astype(F32) * outer
        deg_ref[b : b + 1] = jnp.sum(rows, axis=1, keepdims=True).T
    for b in range(blocks):
        deg_ref[b : b + 1] += acc[b, 0:1]


def send_out(shape, u_ref, w_ref, pattern_ref, terms, pay_refs):
    blocks, slots = w_ref.shape[:2]
    terms[...] = jnp.zeros_like(terms)
    for b in range(RIMS * RIM):
        part = mm(u_ref[b], beside([w_ref[b, s] for s in range(INNER, slots)]), ROWS_BY_COLS)
        base = (b // RIM) * RIM - blocks
        for s in range(INNER, slots):
            i = s - INNER
            terms[base + pattern_ref[s, 0, b]] += part[:, i * LANES : (i + 1) * LANES]
    rim_of, _, _ = places(shape)
    for m in range(4):
        first = rim_of[m] * RIM
        pay_refs[m][0:RIM] = u_ref[pl.ds(first, RIM)]
        pay_refs[m][RIM:] = terms[pl.ds(first, RIM)].astype(BF16)


def first_scaled(shape, pattern_ref, w_ref, deg_ref, x_ref, *refs):
    in_refs, (inv_ref, u_ref), pay_refs, (rims, terms) = refs[:4], refs[4:6], refs[6:10], refs[10:]
    blocks = w_ref.shape[0]
    rim_of, live_of, _ = places(shape)
    for m in range(4):
        rims[rim_of[m]] = in_refs[m][...] * live_of[m].astype(F32)
    for b in range(blocks):
        degree = deg_ref[b : b + 1]
        if b < RIMS * RIM:
            degree = degree + rims[b // RIM, b % RIM : b % RIM + 1]
        inv = 1.0 / jnp.sqrt(0.5 * degree)
        inv_ref[b : b + 1] = inv
        u_ref[b] = (inv * x_ref[:, column(b)].astype(F32)).astype(BF16)
    send_out(shape, u_ref, w_ref, pattern_ref, terms, pay_refs)


def own_products(pattern_ref, w_ref, turned, u_ref, acc_ref):
    blocks, slots = w_ref.shape[:2]
    for b in range(blocks):
        both = mm(u_ref[b], beside([w_ref[b, 0], turned(b, 0)]), ROWS_BY_COLS)
        acc_ref[b] = both[:, :LANES] + both[:, LANES:]
    for b in range(blocks):
        total = None
        own = INNER if b < RIMS * RIM else slots
        for group in slot_pairs(1, own):
            part = mm(u_ref[b], beside([w_ref[b, s] for s in group]), ROWS_BY_COLS)
            for i, s in enumerate(group):
                acc_ref[pattern_ref[s, 0, b]] += part[:, i * LANES : (i + 1) * LANES]
            ahead = beside([u_ref[pattern_ref[s, 0, b]] for s in group])
            ahead = mm(ahead, over([turned(b, s) for s in group]), ROWS_BY_COLS)
            total = ahead if total is None else total + ahead
        acc_ref[b] += total


def own_terms(pattern_ref, w_ref, turned_ref, u_ref, acc_ref):
    own_products(pattern_ref, w_ref, lambda b, s: turned_ref[b, s], u_ref, acc_ref)


def own_terms_turning(pattern_ref, w_ref, u_ref, acc_ref, turned_ref):
    blocks, slots = w_ref.shape[:2]

    def turned(b, s):
        block = w_ref[b, s].T
        turned_ref[b, s] = block
        return block

    own_products(pattern_ref, w_ref, turned, u_ref, acc_ref)
    for b in range(RIMS * RIM):
        for s in range(INNER, slots):
            turned(b, s)


def combine(
    shape, step, pattern_ref, turned_ref, inv_ref, acc_ref, in_refs, y_ref, before_ref, next_ref, ext, u_ref
):
    blocks, slots = turned_ref.shape[:2]
    rim_of, live_of, _ = places(shape)
    for m in range(4):
        ext[pl.ds(rim_of[m] * 2 * RIM, 2 * RIM)] = in_refs[m][...] * live_of[m].astype(BF16)

    def update(b, total):
        inv = inv_ref[b : b + 1]
        y = y_ref[:, column(b)].astype(F32)
        lap = y - inv * (0.5 * total)
        new = (lap - center * y) / half_width
        if step > 0:
            new = 2.0 * new - before_ref[:, column(b)].astype(F32)
        next_ref[:, column(b)] = new
        if u_ref is not None:
            u_ref[b] = (inv * new).astype(BF16)

    for b in range(RIMS * RIM, blocks):
        update(b, acc_ref[b])
    for b in range(RIMS * RIM):
        base = (b // RIM) * 2 * RIM
        ahead = beside([ext[base + pattern_ref[s, 0, b] - blocks] for s in range(INNER, slots)])
        ahead = mm(ahead, over([turned_ref[b, s] for s in range(INNER, slots)]), ROWS_BY_COLS)
        update(b, acc_ref[b] + ahead + ext[base + RIM + b % RIM].astype(F32))


def advance(shape, step, pattern_ref, w_ref, turned_ref, inv_ref, acc_ref, *refs):
    in_refs, (y_ref, before_ref, next_ref, u_ref) = refs[:4], refs[4:8]
    pay_refs, (ext, terms) = refs[8:12], refs[12:]
    combine(
        shape, step, pattern_ref, turned_ref, inv_ref, acc_ref, in_refs, y_ref, before_ref, next_ref, ext, u_ref
    )
    send_out(shape, u_ref, w_ref, pattern_ref, terms, pay_refs)


def finish(shape, pattern_ref, turned_ref, inv_ref, acc_ref, *refs):
    in_refs, (y_ref, before_ref, next_ref, gram_ref, ext) = refs[:4], refs[4:]
    combine(shape, 2, pattern_ref, turned_ref, inv_ref, acc_ref, in_refs, y_ref, before_ref, next_ref, ext, None)
    y = next_ref[...]
    gram = mm(y, y, ROWS_BY_ROWS, lax.Precision.HIGHEST)
    packed = beside([gram[8 * i : 8 * i + 8] for i in range(gram.shape[0] // 8)])
    gram_ref[...] = jnp.broadcast_to(packed[None], gram_ref.shape)


def inverse_factor(gram, scale):
    n = gram.shape[0]
    tall = 8
    groups = range(n // tall)
    lane = lax.broadcasted_iota(jnp.int32, (tall, LANES), 1)
    sub = lax.broadcasted_iota(jnp.int32, (tall, LANES), 0)

    def spread(values, r):
        return jnp.broadcast_to(values[r : r + 1], (tall, LANES))

    both = []
    for i in groups:
        eye = (lane[:, :n] == sub[:, :n] + tall * i).astype(F32)
        both.append(beside([gram[tall * i : tall * (i + 1)], eye, jnp.zeros((tall, LANES - 2 * n), F32)]))
    parts = []
    for q in groups:
        columns = [
            {i: jnp.broadcast_to(both[i][:, tall * q + j : tall * q + j + 1], (tall, LANES)) for i in groups if i >= q}
            for j in range(tall)
        ]
        pivots = None
        for r in range(tall):
            pivot = spread(columns[r][q], r)
            pivots = pivot if pivots is None else jnp.where(sub == r, pivot, pivots)
            inv = 1.0 / pivot
            row = spread(both[q], r) * inv
            below = dict(columns[r])
            below[q] = jnp.where(sub > r, below[q], 0.0)
            live = [i for i in groups if i > q or (i == q and r < tall - 1)]
            for j in range(r + 1, tall):
                scaled = spread(columns[j][q], r) * inv
                for i in live:
                    columns[j][i] = columns[j][i] - below[i] * scaled
            for i in live:
                both[i] = both[i] - below[i] * row
        parts.append((both[q] * (scale / jnp.sqrt(pivots)))[:, n : 2 * n])
    return over(parts)


def orthonormal(scale, grams_ref, y_ref, out_ref):
    packed = jnp.sum(grams_ref[...], axis=0)
    n = y_ref.shape[0]
    gram = over([packed[:, n * i : n * (i + 1)] for i in range(n // 8)])
    out_ref[...] = mm(inverse_factor(gram, scale), y_ref[...], ROWS_BY_COLS, lax.Precision.HIGHEST)


def in_vmem(x):
    return pltpu.with_memory_space_constraint(x, pltpu.VMEM)


def kernel_call(body, name, ins, outs, scratch=(), flops=0, moved=0):
    specs, args = [], []
    for kind, x in ins:
        if kind == "hbm":
            specs.append(pl.BlockSpec(memory_space=pl.ANY))
            x = pltpu.with_memory_space_constraint(x, pltpu.HBM)
        elif kind == "smem":
            specs.append(pl.BlockSpec(memory_space=pltpu.SMEM))
            x = pltpu.with_memory_space_constraint(x, pltpu.SMEM)
        else:
            specs.append(pl.BlockSpec(memory_space=pltpu.VMEM))
            if kind == "held":
                x = in_vmem(x)
        args.append(x)
    return pl.pallas_call(
        body,
        name=name,
        out_shape=[
            pltpu.SMEM(s, d) if d == jnp.int32 else pltpu.VMEM(s, d) if len(s) == 4 else jax.ShapeDtypeStruct(s, d)
            for s, d in outs
        ],
        in_specs=specs,
        out_specs=[pl.BlockSpec(memory_space=pltpu.SMEM if d == jnp.int32 else pltpu.VMEM) for _, d in outs],
        scratch_shapes=list(scratch),
        compiler_params=pltpu.CompilerParams(vmem_limit_bytes=16 << 20),
        cost_estimate=pl.CostEstimate(flops=flops, bytes_accessed=moved, transcendentals=0),
    )(*args)


def swaps():
    tall, broad = lax.axis_size("narrow"), lax.axis_size("wide")
    found = []
    for m in (0, 1):
        pairs = []
        for w in range(broad):
            for i in range(m, tall - 1, 2):
                pairs.append(((i, w), (i + 1, w)))
        if m == 1 and tall <= 4:
            pairs += [((0, w), (tall - 1, w)) for w in range(broad)]
        elif m == 1:
            pairs += [((i, w), (i, w + 1)) for i in (0, tall - 1) for w in range(0, broad, 2)]
        found.append(pairs)
    for m in (0, 1):
        pairs = []
        for i in range(tall):
            for w in range(m, broad - 1, 2):
                pairs.append(((i, w), (i, w + 1)))
        if m == 1:
            pairs += [((i, w), (i + 1, w)) for w in (0, broad - 1) for i in range(0, tall, 2)]
        found.append(pairs)
    flat = []
    for pairs in found:
        ends = [(a[0] * broad + a[1], b[0] * broad + b[1]) for a, b in pairs]
        flat.append([p for a, b in ends for p in ((a, b), (b, a))])
    return flat


def exchange(payloads):
    pairs = swaps()
    return [lax.ppermute(payload, ("narrow", "wide"), pairs[m]) for payload, m in zip(payloads, ORDER)]


def body(start_block, weights, pattern):
    x = start_block[0, 0]
    w = weights[0, 0]
    slots_of = jnp.transpose(pattern, (0, 3, 1, 2))[0]
    shape = (lax.axis_size("narrow"), lax.axis_size("wide"))
    vecs, docs = x.shape
    blocks, slots = w.shape[:2]
    rows = RIMS * RIM
    tile = ((blocks, vecs, LANES), F32)
    scaled = ((blocks, vecs, LANES), BF16)
    full = ((vecs, docs), F32)
    payload = [((2 * RIM, vecs, LANES), BF16)] * 4
    per_block = 2 * LANES * LANES

    *pays, slots_of = kernel_call(
        functools.partial(outgoing_ones, shape), "outgoing_ones", [("hbm", slots_of), ("hbm", w)],
        [((8, LANES), F32)] * 4 + [(slots_of.shape, jnp.int32)],
        [pltpu.VMEM((rows, slots - INNER, LANES, LANES), BF16),
         pltpu.VMEM((rows, 8, LANES), F32), pltpu.SemaphoreType.DMA((RIMS + 1,))],
        flops=rows * 3 * per_block * 32, moved=1 << 20,
    )
    w, *pays = lax.optimization_barrier((w, *pays))
    names = [("smem", slots_of)]
    held = names + [("held", w)]
    (degree,) = kernel_call(
        functools.partial(local_degree, shape), "local_degree", held, [((blocks, LANES), F32)],
        [pltpu.VMEM((blocks, 8, LANES), F32)],
        flops=blocks * slots * per_block * 32, moved=8 << 20,
    )
    got = exchange(pays)
    inv, u, *pays = kernel_call(
        functools.partial(first_scaled, shape), "first_scaled",
        held + [("vmem", degree), ("vmem", x)] + [("vmem", g) for g in got],
        [((blocks, LANES), F32), scaled] + payload,
        [pltpu.VMEM((RIMS, 8, LANES), F32), pltpu.VMEM((rows, vecs, LANES), F32)],
        flops=rows * 3 * per_block * 32, moved=1 << 20,
    )
    before, y = x, x
    for step in range(3):
        cost = dict(flops=2 * blocks * slots * per_block * vecs, moved=8 << 20)
        if step == 0:
            acc, turned = kernel_call(
                own_terms_turning, "own_terms_turning", held + [("vmem", u)], [tile, (w.shape, BF16)],
                **cost
            )
        else:
            (acc,) = kernel_call(
                own_terms, "own_terms", held + [("held", turned), ("vmem", u)], [tile], **cost
            )
        got = exchange(pays)
        common = [("held", turned), ("vmem", inv), ("vmem", acc)] + [("vmem", g) for g in got]
        common += [("vmem", y), ("vmem", before)]
        ext = pltpu.VMEM((2 * rows, vecs, LANES), BF16)
        if step < 2:
            new, u, *pays = kernel_call(
                functools.partial(advance, shape, step), "advance", held + common, [full, scaled] + payload,
                [ext, pltpu.VMEM((rows, vecs, LANES), F32)],
                flops=2 * rows * 3 * per_block * 32, moved=1 << 20,
            )
        else:
            peers = shape[0] * shape[1]
            new, grams = kernel_call(
                functools.partial(finish, shape), "finish", names + common, [full, ((peers, 8, LANES), F32)],
                [ext],
                flops=rows * 3 * per_block * 32, moved=1 << 20,
            )
        before, y = y, new
    grams = lax.all_to_all(grams, ("narrow", "wide"), 0, 0)
    (out,) = kernel_call(
        functools.partial(orthonormal, math.sqrt(peers * docs)), "orthonormal",
        [("vmem", grams), ("vmem", y)], [full],
    )
    return out[None, None]


def solution(mesh):
    placed = (
        P("narrow", "wide", None, None),
        P("narrow", "wide", None, None, None, None),
        P("narrow", "wide", None, None),
    )
    return jax.shard_map(
        body, mesh=mesh, in_specs=placed, out_specs=P("narrow", "wide", None, None), check_vma=False
    )
```

```python
import functools
import math

import jax
import jax.numpy as jnp
from jax import lax
from jax.experimental import pallas as pl
from jax.experimental.pallas import tpu as pltpu
from jax.sharding import PartitionSpec as P

RIM = 6
RIMS = 4
INNER = 9
PARTS = 3
LANES = 128
F32 = jnp.float32
BF16 = jnp.bfloat16

lower_edge = 0.3
center = (2.0 + lower_edge) / 2.0
half_width = (2.0 - lower_edge) / 2.0

ROWS_BY_ROWS = (((1,), (1,)), ((), ()))
ROWS_BY_COLS = (((1,), (0,)), ((), ()))


def mm(left, right, dims):
    return lax.dot_general(left, right, dims, preferred_element_type=F32)


def three(x):
    high = x.astype(BF16)
    rest = x - high.astype(F32)
    mid = rest.astype(BF16)
    return high, mid, (rest - mid.astype(F32)).astype(BF16)


def beside(parts):
    return parts[0] if len(parts) == 1 else jnp.concatenate(parts, axis=1)


def over(parts):
    return parts[0] if len(parts) == 1 else jnp.concatenate(parts, axis=0)


def slot_pairs(first, last):
    return [list(range(s, min(s + 2, last))) for s in range(first, last, 2)]


def column(b):
    return pl.ds(b * LANES, LANES)


ORDER = (2, 3, 1, 0)


def places(shape):
    rim_of, live_of, by_rim = [], [], []
    for a, axis in enumerate(("narrow", "wide")):
        place = lax.axis_index(axis)
        behind = (place > 0).astype(jnp.int32)
        ahead = (place < shape[a] - 1).astype(jnp.int32)
        odd = lax.rem(place, 2)
        for m in (0, 1):
            after = odd if m else 1 - odd
            rim_of.append(2 * a + after)
            live_of.append(after * ahead + (1 - after) * behind)
        by_rim += [behind, ahead]
    return [rim_of[m] for m in ORDER], [live_of[m] for m in ORDER], by_rim


def fetch(source, target, sem):
    copy = pltpu.make_async_copy(source, target, sem)
    copy.start()
    return copy


def outgoing_ones(shape, pattern_hbm, w_hbm, *refs):
    pay_refs, (pattern_ref, w_ref, sums, sems) = refs[:4], refs[4:]
    named = fetch(pattern_hbm, pattern_ref, sems.at[PARTS])
    copies = []
    for part in range(PARTS):
        rows = pl.ds(part * RIMS * RIM // PARTS, RIMS * RIM // PARTS)
        copies.append(fetch(w_hbm.at[rows, INNER:], w_ref.at[rows], sems.at[part]))
    blocks = pattern_ref.shape[2]
    slots = w_ref.shape[1]
    sums[...] = jnp.zeros_like(sums)
    ones = jnp.ones((8, LANES), BF16)
    named.wait()
    for p in range(PARTS):
        copies[p].wait()
        for b in range(p * RIMS * RIM // PARTS, (p + 1) * RIMS * RIM // PARTS):
            part = mm(ones, beside([w_ref[b, s] for s in range(slots)]), ROWS_BY_COLS)
            for s in range(slots):
                sums[b // RIM * RIM - blocks + pattern_ref[INNER + s, 0, b]] += part[:, s * LANES : (s + 1) * LANES]
    rim_of, _, _ = places(shape)
    for m in range(4):
        for q in range(RIM):
            pay_refs[m][q : q + 1] = sums[rim_of[m] * RIM + q][0:1].astype(BF16).astype(F32)


def local_degree(shape, pattern_ref, w_ref, deg_ref, acc):
    blocks, slots = w_ref.shape[:2]
    by_rim = places(shape)[2]
    ones = jnp.ones((8, LANES), BF16)
    for b in range(0, blocks, 2):
        part = mm(ones, beside([w_ref[b, 0], w_ref[b + 1, 0]]), ROWS_BY_COLS)
        acc[b] = part[:, :LANES]
        acc[b + 1] = part[:, LANES:]
    for b in range(blocks):
        own = INNER if b < RIMS * RIM else slots
        for group in slot_pairs(1, own):
            part = mm(ones, beside([w_ref[b, s] for s in group]), ROWS_BY_COLS)
            for i, s in enumerate(group):
                acc[pattern_ref[s, 0, b]] += part[:, i * LANES : (i + 1) * LANES]
        rows = w_ref[b, 0].astype(F32)
        for s in range(1, own):
            rows = rows + w_ref[b, s].astype(F32)
        if own < slots:
            outer = w_ref[b, own].astype(F32)
            for s in range(own + 1, slots):
                outer = outer + w_ref[b, s].astype(F32)
            rows = rows + by_rim[b // RIM].astype(F32) * outer
        deg_ref[b : b + 1] = jnp.sum(rows, axis=1, keepdims=True).T
    for b in range(blocks):
        deg_ref[b : b + 1] += acc[b, 0:1]


def send_out(shape, u_ref, w_ref, pattern_ref, terms, pay_refs):
    blocks, slots = w_ref.shape[:2]
    terms[...] = jnp.zeros_like(terms)
    for b in range(RIMS * RIM):
        part = mm(u_ref[b], beside([w_ref[b, s] for s in range(INNER, slots)]), ROWS_BY_COLS)
        base = (b // RIM) * RIM - blocks
        for s in range(INNER, slots):
            i = s - INNER
            terms[base + pattern_ref[s, 0, b]] += part[:, i * LANES : (i + 1) * LANES]
    rim_of, _, _ = places(shape)
    for m in range(4):
        first = rim_of[m] * RIM
        pay_refs[m][0:RIM] = u_ref[pl.ds(first, RIM)]
        pay_refs[m][RIM:] = terms[pl.ds(first, RIM)].astype(BF16)


def first_scaled(shape, pattern_ref, w_ref, deg_ref, x_ref, *refs):
    in_refs, (inv_ref, u_ref), pay_refs, (rims, terms) = refs[:4], refs[4:6], refs[6:10], refs[10:]
    blocks = w_ref.shape[0]
    rim_of, live_of, _ = places(shape)
    for m in range(4):
        rims[rim_of[m]] = in_refs[m][...] * live_of[m].astype(F32)
    for b in range(blocks):
        degree = deg_ref[b : b + 1]
        if b < RIMS * RIM:
            degree = degree + rims[b // RIM, b % RIM : b % RIM + 1]
        inv = 1.0 / jnp.sqrt(0.5 * degree)
        inv_ref[b : b + 1] = inv
        u_ref[b] = (inv * x_ref[:, column(b)].astype(F32)).astype(BF16)
    send_out(shape, u_ref, w_ref, pattern_ref, terms, pay_refs)


def own_products(pattern_ref, w_ref, turned, u_ref, acc_ref):
    blocks, slots = w_ref.shape[:2]
    for b in range(blocks):
        both = mm(u_ref[b], beside([w_ref[b, 0], turned(b, 0)]), ROWS_BY_COLS)
        acc_ref[b] = both[:, :LANES] + both[:, LANES:]
    for b in range(blocks):
        total = None
        own = INNER if b < RIMS * RIM else slots
        for group in slot_pairs(1, own):
            part = mm(u_ref[b], beside([w_ref[b, s] for s in group]), ROWS_BY_COLS)
            for i, s in enumerate(group):
                acc_ref[pattern_ref[s, 0, b]] += part[:, i * LANES : (i + 1) * LANES]
            ahead = beside([u_ref[pattern_ref[s, 0, b]] for s in group])
            ahead = mm(ahead, over([turned(b, s) for s in group]), ROWS_BY_COLS)
            total = ahead if total is None else total + ahead
        acc_ref[b] += total


def own_terms(pattern_ref, w_ref, turned_ref, u_ref, acc_ref):
    own_products(pattern_ref, w_ref, lambda b, s: turned_ref[b, s], u_ref, acc_ref)


def own_terms_turning(pattern_ref, w_ref, u_ref, acc_ref, turned_ref):
    blocks, slots = w_ref.shape[:2]

    def turned(b, s):
        block = w_ref[b, s].T
        turned_ref[b, s] = block
        return block

    own_products(pattern_ref, w_ref, turned, u_ref, acc_ref)
    for b in range(RIMS * RIM):
        for s in range(INNER, slots):
            turned(b, s)


def combine(
    shape, step, pattern_ref, turned_ref, inv_ref, acc_ref, in_refs, y_ref, before_ref, next_ref, ext, u_ref
):
    blocks, slots = turned_ref.shape[:2]
    rim_of, live_of, _ = places(shape)
    for m in range(4):
        ext[pl.ds(rim_of[m] * 2 * RIM, 2 * RIM)] = in_refs[m][...] * live_of[m].astype(BF16)

    def update(b, total):
        inv = inv_ref[b : b + 1]
        y = y_ref[:, column(b)].astype(F32)
        lap = y - inv * (0.5 * total)
        new = (lap - center * y) / half_width
        if step > 0:
            new = 2.0 * new - before_ref[:, column(b)].astype(F32)
        next_ref[:, column(b)] = new
        if u_ref is not None:
            u_ref[b] = (inv * new).astype(BF16)

    for b in range(RIMS * RIM, blocks):
        update(b, acc_ref[b])
    for b in range(RIMS * RIM):
        base = (b // RIM) * 2 * RIM
        ahead = beside([ext[base + pattern_ref[s, 0, b] - blocks] for s in range(INNER, slots)])
        ahead = mm(ahead, over([turned_ref[b, s] for s in range(INNER, slots)]), ROWS_BY_COLS)
        update(b, acc_ref[b] + ahead + ext[base + RIM + b % RIM].astype(F32))


def advance(shape, step, pattern_ref, w_ref, turned_ref, inv_ref, acc_ref, *refs):
    in_refs, (y_ref, before_ref, next_ref, u_ref) = refs[:4], refs[4:8]
    pay_refs, (ext, terms) = refs[8:12], refs[12:]
    combine(
        shape, step, pattern_ref, turned_ref, inv_ref, acc_ref, in_refs, y_ref, before_ref, next_ref, ext, u_ref
    )
    send_out(shape, u_ref, w_ref, pattern_ref, terms, pay_refs)


def finish(shape, pattern_ref, turned_ref, inv_ref, acc_ref, *refs):
    in_refs, (y_ref, before_ref, next_ref, gram_ref, ext) = refs[:4], refs[4:]
    combine(shape, 2, pattern_ref, turned_ref, inv_ref, acc_ref, in_refs, y_ref, before_ref, next_ref, ext, None)
    n = next_ref.shape[0]
    terms = over(three(next_ref[...]))
    every = mm(terms, terms, ROWS_BY_ROWS)
    gram = sum(every[n * i : n * (i + 1), n * j : n * (j + 1)] for i, j in ((0, 2), (2, 0), (1, 1), (0, 1), (1, 0), (0, 0)))
    packed = beside([gram[8 * i : 8 * i + 8] for i in range(gram.shape[0] // 8)])
    gram_ref[...] = jnp.broadcast_to(packed[None], gram_ref.shape)


def inverse_factor(gram, scale):
    n = gram.shape[0]
    tall = 8
    groups = range(n // tall)
    lane = lax.broadcasted_iota(jnp.int32, (tall, LANES), 1)
    sub = lax.broadcasted_iota(jnp.int32, (tall, LANES), 0)

    def spread(values, r):
        return jnp.broadcast_to(values[r : r + 1], (tall, LANES))

    both = []
    for i in groups:
        eye = (lane[:, :n] == sub[:, :n] + tall * i).astype(F32)
        both.append(beside([gram[tall * i : tall * (i + 1)], eye, jnp.zeros((tall, LANES - 2 * n), F32)]))
    parts = []
    for q in groups:
        columns = [
            {i: jnp.broadcast_to(both[i][:, tall * q + j : tall * q + j + 1], (tall, LANES)) for i in groups if i >= q}
            for j in range(tall)
        ]
        pivots = None
        for r in range(tall):
            pivot = spread(columns[r][q], r)
            pivots = pivot if pivots is None else jnp.where(sub == r, pivot, pivots)
            inv = 1.0 / pivot
            row = spread(both[q], r) * inv
            below = dict(columns[r])
            below[q] = jnp.where(sub > r, below[q], 0.0)
            live = [i for i in groups if i > q or (i == q and r < tall - 1)]
            for j in range(r + 1, tall):
                scaled = spread(columns[j][q], r) * inv
                for i in live:
                    columns[j][i] = columns[j][i] - below[i] * scaled
            for i in live:
                both[i] = both[i] - below[i] * row
        parts.append((both[q] * (scale / jnp.sqrt(pivots)))[:, n : 2 * n])
    return over(parts)


def orthonormal(scale, grams_ref, y_ref, out_ref):
    packed = jnp.sum(grams_ref[...], axis=0)
    n = y_ref.shape[0]
    gram = over([packed[:, n * i : n * (i + 1)] for i in range(n // 8)])
    a = three(inverse_factor(gram, scale))
    pairs = ((0, 0), (0, 1), (1, 0), (0, 2), (1, 1), (2, 0))
    left = beside([a[i] for i, _ in pairs])
    width = 4 * LANES
    for at in range(0, y_ref.shape[1], width):
        y = three(y_ref[:, at : at + width])
        out_ref[:, at : at + width] = mm(left, over([y[j] for _, j in pairs]), ROWS_BY_COLS)


def in_vmem(x):
    return pltpu.with_memory_space_constraint(x, pltpu.VMEM)


def kernel_call(body, name, ins, outs, scratch=(), flops=0, moved=0):
    specs, args = [], []
    for kind, x in ins:
        if kind == "hbm":
            specs.append(pl.BlockSpec(memory_space=pl.ANY))
            x = pltpu.with_memory_space_constraint(x, pltpu.HBM)
        elif kind == "smem":
            specs.append(pl.BlockSpec(memory_space=pltpu.SMEM))
            x = pltpu.with_memory_space_constraint(x, pltpu.SMEM)
        else:
            specs.append(pl.BlockSpec(memory_space=pltpu.VMEM))
            if kind == "held":
                x = in_vmem(x)
        args.append(x)
    return pl.pallas_call(
        body,
        name=name,
        out_shape=[
            pltpu.SMEM(s, d) if d == jnp.int32 else pltpu.VMEM(s, d) if len(s) == 4 else jax.ShapeDtypeStruct(s, d)
            for s, d in outs
        ],
        in_specs=specs,
        out_specs=[pl.BlockSpec(memory_space=pltpu.SMEM if d == jnp.int32 else pltpu.VMEM) for _, d in outs],
        scratch_shapes=list(scratch),
        compiler_params=pltpu.CompilerParams(vmem_limit_bytes=16 << 20),
        cost_estimate=pl.CostEstimate(flops=flops, bytes_accessed=moved, transcendentals=0),
    )(*args)


def swaps():
    tall, broad = lax.axis_size("narrow"), lax.axis_size("wide")
    found = []
    for m in (0, 1):
        pairs = []
        for w in range(broad):
            for i in range(m, tall - 1, 2):
                pairs.append(((i, w), (i + 1, w)))
        if m == 1 and tall <= 4:
            pairs += [((0, w), (tall - 1, w)) for w in range(broad)]
        elif m == 1:
            pairs += [((i, w), (i, w + 1)) for i in (0, tall - 1) for w in range(0, broad, 2)]
        found.append(pairs)
    for m in (0, 1):
        pairs = []
        for i in range(tall):
            for w in range(m, broad - 1, 2):
                pairs.append(((i, w), (i, w + 1)))
        if m == 1:
            pairs += [((i, w), (i + 1, w)) for w in (0, broad - 1) for i in range(0, tall, 2)]
        found.append(pairs)
    flat = []
    for pairs in found:
        ends = [(a[0] * broad + a[1], b[0] * broad + b[1]) for a, b in pairs]
        flat.append([p for a, b in ends for p in ((a, b), (b, a))])
    return flat


def exchange(payloads):
    pairs = swaps()
    return [lax.ppermute(payload, ("narrow", "wide"), pairs[m]) for payload, m in zip(payloads, ORDER)]


def body(start_block, weights, pattern):
    x = start_block[0, 0]
    w = weights[0, 0]
    slots_of = jnp.transpose(pattern, (0, 3, 1, 2))[0]
    shape = (lax.axis_size("narrow"), lax.axis_size("wide"))
    vecs, docs = x.shape
    blocks, slots = w.shape[:2]
    rows = RIMS * RIM
    tile = ((blocks, vecs, LANES), F32)
    scaled = ((blocks, vecs, LANES), BF16)
    full = ((vecs, docs), F32)
    payload = [((2 * RIM, vecs, LANES), BF16)] * 4
    per_block = 2 * LANES * LANES

    *pays, slots_of = kernel_call(
        functools.partial(outgoing_ones, shape), "outgoing_ones", [("hbm", slots_of), ("hbm", w)],
        [((8, LANES), F32)] * 4 + [(slots_of.shape, jnp.int32)],
        [pltpu.VMEM((rows, slots - INNER, LANES, LANES), BF16),
         pltpu.VMEM((rows, 8, LANES), F32), pltpu.SemaphoreType.DMA((PARTS + 1,))],
        flops=rows * 3 * per_block * 32, moved=1 << 20,
    )
    w, *pays = lax.optimization_barrier((w, *pays))
    names = [("smem", slots_of)]
    held = names + [("held", w)]
    (degree,) = kernel_call(
        functools.partial(local_degree, shape), "local_degree", held, [((blocks, LANES), F32)],
        [pltpu.VMEM((blocks, 8, LANES), F32)],
        flops=blocks * slots * per_block * 32, moved=8 << 20,
    )
    got = exchange(pays)
    inv, u, *pays = kernel_call(
        functools.partial(first_scaled, shape), "first_scaled",
        held + [("vmem", degree), ("vmem", x)] + [("vmem", g) for g in got],
        [((blocks, LANES), F32), scaled] + payload,
        [pltpu.VMEM((RIMS, 8, LANES), F32), pltpu.VMEM((rows, vecs, LANES), F32)],
        flops=rows * 3 * per_block * 32, moved=1 << 20,
    )
    before, y = x, x
    for step in range(3):
        cost = dict(flops=2 * blocks * slots * per_block * vecs, moved=8 << 20)
        if step == 0:
            acc, turned = kernel_call(
                own_terms_turning, "own_terms_turning", held + [("vmem", u)], [tile, (w.shape, BF16)],
                **cost
            )
        else:
            (acc,) = kernel_call(
                own_terms, "own_terms", held + [("held", turned), ("vmem", u)], [tile], **cost
            )
        got = exchange(pays)
        common = [("held", turned), ("vmem", inv), ("vmem", acc)] + [("vmem", g) for g in got]
        common += [("vmem", y), ("vmem", before)]
        ext = pltpu.VMEM((2 * rows, vecs, LANES), BF16)
        if step < 2:
            new, u, *pays = kernel_call(
                functools.partial(advance, shape, step), "advance", held + common, [full, scaled] + payload,
                [ext, pltpu.VMEM((rows, vecs, LANES), F32)],
                flops=2 * rows * 3 * per_block * 32, moved=1 << 20,
            )
        else:
            peers = shape[0] * shape[1]
            new, grams = kernel_call(
                functools.partial(finish, shape), "finish", names + common, [full, ((peers, 8, LANES), F32)],
                [ext],
                flops=rows * 3 * per_block * 32, moved=1 << 20,
            )
        before, y = y, new
    grams = lax.all_to_all(grams, ("narrow", "wide"), 0, 0)
    (out,) = kernel_call(
        functools.partial(orthonormal, math.sqrt(peers * docs)), "orthonormal",
        [("vmem", grams), ("vmem", y)], [full],
    )
    return out[None, None]


def solution(mesh):
    placed = (
        P("narrow", "wide", None, None),
        P("narrow", "wide", None, None, None, None),
        P("narrow", "wide", None, None),
    )
    return jax.shard_map(
        body, mesh=mesh, in_specs=placed, out_specs=P("narrow", "wide", None, None), check_vma=False
    )
```

```python
import functools
import math

import jax
import jax.numpy as jnp
from jax import lax
from jax.experimental import pallas as pl
from jax.experimental.pallas import tpu as pltpu
from jax.sharding import PartitionSpec as P

RIM = 6
RIMS = 4
INNER = 9
PARTS = 3
LANES = 128
F32 = jnp.float32
BF16 = jnp.bfloat16

lower_edge = 0.3
center = (2.0 + lower_edge) / 2.0
half_width = (2.0 - lower_edge) / 2.0

ROWS_BY_ROWS = (((1,), (1,)), ((), ()))
ROWS_BY_COLS = (((1,), (0,)), ((), ()))


def mm(left, right, dims):
    return lax.dot_general(left, right, dims, preferred_element_type=F32)


def three(x):
    high = x.astype(BF16)
    rest = x - high.astype(F32)
    mid = rest.astype(BF16)
    return high, mid, (rest - mid.astype(F32)).astype(BF16)


def beside(parts):
    return parts[0] if len(parts) == 1 else jnp.concatenate(parts, axis=1)


def over(parts):
    return parts[0] if len(parts) == 1 else jnp.concatenate(parts, axis=0)


def slot_pairs(first, last):
    return [list(range(s, min(s + 2, last))) for s in range(first, last, 2)]


def column(b):
    return pl.ds(b * LANES, LANES)


ORDER = (2, 3, 1, 0)


def places(shape):
    rim_of, live_of, by_rim = [], [], []
    for a, axis in enumerate(("narrow", "wide")):
        place = lax.axis_index(axis)
        behind = (place > 0).astype(jnp.int32)
        ahead = (place < shape[a] - 1).astype(jnp.int32)
        odd = lax.rem(place, 2)
        for m in (0, 1):
            after = odd if m else 1 - odd
            rim_of.append(2 * a + after)
            live_of.append(after * ahead + (1 - after) * behind)
        by_rim += [behind, ahead]
    return [rim_of[m] for m in ORDER], [live_of[m] for m in ORDER], by_rim


def fetch(source, target, sem):
    copy = pltpu.make_async_copy(source, target, sem)
    copy.start()
    return copy


def outgoing_ones(shape, pattern_hbm, w_hbm, *refs):
    pay_refs, (pattern_ref, w_ref, sems), sums = refs[:4], refs[4:7], refs[7:]
    named = fetch(pattern_hbm, pattern_ref, sems.at[PARTS])
    copies = []
    for part in range(PARTS):
        rows = pl.ds(part * RIMS * RIM // PARTS, RIMS * RIM // PARTS)
        copies.append(fetch(w_hbm.at[rows, INNER:], w_ref.at[rows], sems.at[part]))
    blocks = pattern_ref.shape[2]
    slots = w_ref.shape[1]
    for r in range(RIMS):
        sums[r][...] = jnp.zeros_like(sums[r])
    ones = jnp.ones((8, LANES), BF16)
    named.wait()
    for p in range(PARTS):
        copies[p].wait()
        for b in range(p * RIMS * RIM // PARTS, (p + 1) * RIMS * RIM // PARTS):
            part = mm(ones, beside([w_ref[b, s] for s in range(slots)]), ROWS_BY_COLS)
            for s in range(slots):
                sums[b // RIM][pattern_ref[INNER + s, 0, b] - blocks] += part[:, s * LANES : (s + 1) * LANES]
    rim_of, _, _ = places(shape)
    for m in range(4):
        low = ORDER[m] // 2 * 2
        upper = (rim_of[m] - low).astype(F32)
        for q in range(RIM):
            total = sums[low][q, 0:1] * (1.0 - upper) + sums[low + 1][q, 0:1] * upper
            pay_refs[m][q : q + 1] = total.astype(BF16).astype(F32)


def local_degree(shape, pattern_ref, w_ref, deg_ref, *accs):
    blocks, slots = w_ref.shape[:2]
    by_rim = places(shape)[2]
    ones = jnp.ones((8, LANES), BF16)
    for b in range(0, blocks, 2):
        part = mm(ones, beside([w_ref[b, 0], w_ref[b + 1, 0]]), ROWS_BY_COLS)
        accs[0][b] = part[:, :LANES]
        accs[0][b + 1] = part[:, LANES:]
    for acc in accs[1:]:
        acc[...] = jnp.zeros_like(acc)
    for b in range(blocks):
        own = INNER if b < RIMS * RIM else slots
        for group in slot_pairs(1, own):
            part = mm(ones, beside([w_ref[b, s] for s in group]), ROWS_BY_COLS)
            for i, s in enumerate(group):
                accs[s % len(accs)][pattern_ref[s, 0, b]] += part[:, i * LANES : (i + 1) * LANES]
        rows = w_ref[b, 0].astype(F32)
        for s in range(1, own):
            rows = rows + w_ref[b, s].astype(F32)
        if own < slots:
            outer = w_ref[b, own].astype(F32)
            for s in range(own + 1, slots):
                outer = outer + w_ref[b, s].astype(F32)
            rows = rows + by_rim[b // RIM].astype(F32) * outer
        deg_ref[b : b + 1] = jnp.sum(rows, axis=1, keepdims=True).T
    for b in range(blocks):
        deg_ref[b : b + 1] += sum(acc[b, 0:1] for acc in accs)


def halves(blocks):
    wide = tuple(range(2 * RIM, RIMS * RIM))
    return wide, tuple(b for b in range(blocks) if b not in wide)


def first_rim(half):
    return 2 - 2 * half


def send_out(shape, half, u_ref, w_ref, pattern_ref, terms, pay_refs):
    blocks, slots = w_ref.shape[:2]
    terms[...] = jnp.zeros_like(terms)
    for i in range(2 * RIM):
        b = first_rim(half) * RIM + i
        part = mm(u_ref[i], beside([w_ref[b, s] for s in range(INNER, slots)]), ROWS_BY_COLS)
        base = i // RIM * RIM - blocks
        for s in range(INNER, slots):
            at = s - INNER
            terms[base + pattern_ref[s, 0, b]] += part[:, at * LANES : (at + 1) * LANES]
    rim_of, _, _ = places(shape)
    for k in range(2):
        first = (rim_of[2 * half + k] - first_rim(half)) * RIM
        pay_refs[k][0:RIM] = u_ref[pl.ds(first, RIM)]
        pay_refs[k][RIM:] = terms[pl.ds(first, RIM)].astype(BF16)


def first_scaled(shape, half, pattern_ref, w_ref, deg_ref, x_ref, *refs):
    in_refs, (inv_ref, u_ref), pay_refs, (rims, terms) = refs[:2], refs[2:4], refs[4:6], refs[6:]
    rim_of, live_of, _ = places(shape)
    for k in range(2):
        m = 2 * half + k
        rims[rim_of[m] - first_rim(half)] = in_refs[k][...] * live_of[m].astype(F32)
    for i, b in enumerate(halves(w_ref.shape[0])[half]):
        degree = deg_ref[b : b + 1]
        if b < RIMS * RIM:
            degree = degree + rims[i // RIM, b % RIM : b % RIM + 1]
        inv = 1.0 / jnp.sqrt(0.5 * degree)
        inv_ref[i : i + 1] = inv
        u_ref[i] = (inv * x_ref[:, column(b)].astype(F32)).astype(BF16)
    send_out(shape, half, u_ref, w_ref, pattern_ref, terms, pay_refs)


def gather_halves(u_refs, u):
    for part_ref, blocks in zip(u_refs, halves(u.shape[0])):
        for i, b in enumerate(blocks):
            u[b] = part_ref[i]


def own_products(pattern_ref, w_ref, turned, u_ref, acc_ref):
    blocks, slots = w_ref.shape[:2]
    for b in range(blocks):
        both = mm(u_ref[b], beside([w_ref[b, 0], turned(b, 0)]), ROWS_BY_COLS)
        acc_ref[b] = both[:, :LANES] + both[:, LANES:]
    for b in range(blocks):
        total = None
        own = INNER if b < RIMS * RIM else slots
        for group in slot_pairs(1, own):
            part = mm(u_ref[b], beside([w_ref[b, s] for s in group]), ROWS_BY_COLS)
            for i, s in enumerate(group):
                acc_ref[pattern_ref[s, 0, b]] += part[:, i * LANES : (i + 1) * LANES]
            ahead = beside([u_ref[pattern_ref[s, 0, b]] for s in group])
            ahead = mm(ahead, over([turned(b, s) for s in group]), ROWS_BY_COLS)
            total = ahead if total is None else total + ahead
        acc_ref[b] += total


def own_terms(pattern_ref, w_ref, turned_ref, u_wide, u_rest, acc_ref, u):
    gather_halves((u_wide, u_rest), u)
    own_products(pattern_ref, w_ref, lambda b, s: turned_ref[b, s], u, acc_ref)


def own_terms_turning(pattern_ref, w_ref, u_wide, u_rest, acc_ref, turned_ref, u):
    blocks, slots = w_ref.shape[:2]

    def turned(b, s):
        block = w_ref[b, s].T
        turned_ref[b, s] = block
        return block

    gather_halves((u_wide, u_rest), u)
    own_products(pattern_ref, w_ref, turned, u, acc_ref)
    for b in range(RIMS * RIM):
        for s in range(INNER, slots):
            turned(b, s)


def combine(shape, step, half, pattern_ref, turned_ref, inv_ref, acc_ref, in_refs, y_ref, before_ref, ext, write):
    blocks, slots = turned_ref.shape[:2]
    rim_of, live_of, _ = places(shape)
    for k in range(2):
        m = 2 * half + k
        first = (rim_of[m] - first_rim(half)) * 2 * RIM
        ext[pl.ds(first, 2 * RIM)] = in_refs[k][...] * live_of[m].astype(BF16)
    mine = halves(blocks)[half]

    def vectors(ref, b, i):
        whole = ref.shape[1] == blocks * LANES
        return ref[:, column(b if whole else i)].astype(F32)

    def update(b, i, total):
        inv = inv_ref[i : i + 1]
        y = vectors(y_ref, b, i)
        lap = y - inv * (0.5 * total)
        new = (lap - center * y) / half_width
        if step > 0:
            new = 2.0 * new - vectors(before_ref, b, i)
        write(b, i, new, inv)

    for i in range(2 * RIM, len(mine)):
        update(mine[i], i, acc_ref[mine[i]])
    for i in range(2 * RIM):
        b = mine[i]
        base = i // RIM * 2 * RIM
        ahead = beside([ext[base + pattern_ref[s, 0, b] - blocks] for s in range(INNER, slots)])
        ahead = mm(ahead, over([turned_ref[b, s] for s in range(INNER, slots)]), ROWS_BY_COLS)
        update(b, i, acc_ref[b] + ahead + ext[base + RIM + b % RIM].astype(F32))


def advance(shape, step, half, pattern_ref, w_ref, turned_ref, inv_ref, acc_ref, *refs):
    in_refs, (y_ref, before_ref, next_ref, u_ref), pay_refs, (ext, terms) = refs[:2], refs[2:6], refs[6:8], refs[8:]

    def write(b, i, new, inv):
        next_ref[:, column(i)] = new
        u_ref[i] = (inv * new).astype(BF16)

    combine(
        shape, step, half, pattern_ref, turned_ref, inv_ref, acc_ref, in_refs, y_ref, before_ref, ext, write
    )
    send_out(shape, half, u_ref, w_ref, pattern_ref, terms, pay_refs)


def finish(shape, half, pattern_ref, turned_ref, inv_ref, acc_ref, *refs):
    in_refs, (y_ref, before_ref), refs = refs[:2], refs[2:4], refs[4:]
    next_ref, gram_ref, ext = refs[-3:]

    def write(b, i, new, inv):
        next_ref[:, column(i)] = new

    combine(shape, 2, half, pattern_ref, turned_ref, inv_ref, acc_ref, in_refs, y_ref, before_ref, ext, write)
    n = next_ref.shape[0]
    terms = over(three(next_ref[...]))
    every = mm(terms, terms, ROWS_BY_ROWS)
    gram = sum(every[n * i : n * (i + 1), n * j : n * (j + 1)] for i, j in ((0, 2), (2, 0), (1, 1), (0, 1), (1, 0), (0, 0)))
    packed = beside([gram[8 * i : 8 * i + 8] for i in range(n // 8)])
    if half == 0:
        gram_ref[...] = packed
    else:
        gram_ref[...] = jnp.broadcast_to((packed + refs[0][...])[None], gram_ref.shape)


def inverse_factor(gram, scale):
    n = gram.shape[0]
    tall = 8
    groups = range(n // tall)
    lane = lax.broadcasted_iota(jnp.int32, (tall, LANES), 1)
    sub = lax.broadcasted_iota(jnp.int32, (tall, LANES), 0)

    def spread(values, r):
        return jnp.broadcast_to(values[r : r + 1], (tall, LANES))

    both = []
    for i in groups:
        eye = (lane[:, :n] == sub[:, :n] + tall * i).astype(F32)
        both.append(beside([gram[tall * i : tall * (i + 1)], eye, jnp.zeros((tall, LANES - 2 * n), F32)]))
    parts = []
    for q in groups:
        columns = [
            {i: jnp.broadcast_to(both[i][:, tall * q + j : tall * q + j + 1], (tall, LANES)) for i in groups if i >= q}
            for j in range(tall)
        ]
        pivots = None
        for r in range(tall):
            pivot = spread(columns[r][q], r)
            pivots = pivot if pivots is None else jnp.where(sub == r, pivot, pivots)
            inv = 1.0 / pivot
            row = spread(both[q], r) * inv
            below = dict(columns[r])
            below[q] = jnp.where(sub > r, below[q], 0.0)
            live = [i for i in groups if i > q or (i == q and r < tall - 1)]
            for j in range(r + 1, tall):
                scaled = spread(columns[j][q], r) * inv
                for i in live:
                    columns[j][i] = columns[j][i] - below[i] * scaled
            for i in live:
                both[i] = both[i] - below[i] * row
        parts.append((both[q] * (scale / jnp.sqrt(pivots)))[:, n : 2 * n])
    return over(parts)


def orthonormal(scale, grams_ref, wide_ref, rest_ref, out_ref):
    packed = jnp.sum(grams_ref[...], axis=0)
    n = wide_ref.shape[0]
    gram = over([packed[:, n * i : n * (i + 1)] for i in range(n // 8)])
    a = three(inverse_factor(gram, scale))
    pairs = ((0, 0), (0, 1), (1, 0), (0, 2), (1, 1), (2, 0))
    left = beside([a[i] for i, _ in pairs])
    width = 4 * LANES
    at = 0
    for ref, first in ((rest_ref, 0), (wide_ref, 0), (rest_ref, 2 * RIM * LANES)):
        last = 2 * RIM * LANES if first == 0 else ref.shape[1]
        for start in range(first, last, width):
            y = three(ref[:, start : start + width])
            out_ref[:, at : at + width] = mm(left, over([y[j] for _, j in pairs]), ROWS_BY_COLS)
            at += width


def in_vmem(x):
    return pltpu.with_memory_space_constraint(x, pltpu.VMEM)


def kernel_call(body, name, ins, outs, scratch=(), flops=0, moved=0):
    specs, args = [], []
    for kind, x in ins:
        if kind == "hbm":
            specs.append(pl.BlockSpec(memory_space=pl.ANY))
            x = pltpu.with_memory_space_constraint(x, pltpu.HBM)
        elif kind == "smem":
            specs.append(pl.BlockSpec(memory_space=pltpu.SMEM))
            x = pltpu.with_memory_space_constraint(x, pltpu.SMEM)
        else:
            specs.append(pl.BlockSpec(memory_space=pltpu.VMEM))
            if kind == "held":
                x = in_vmem(x)
        args.append(x)
    return pl.pallas_call(
        body,
        name=name,
        out_shape=[
            pltpu.SMEM(s, d) if d == jnp.int32 else pltpu.VMEM(s, d) if len(s) == 4 else jax.ShapeDtypeStruct(s, d)
            for s, d in outs
        ],
        in_specs=specs,
        out_specs=[pl.BlockSpec(memory_space=pltpu.SMEM if d == jnp.int32 else pltpu.VMEM) for _, d in outs],
        scratch_shapes=list(scratch),
        compiler_params=pltpu.CompilerParams(vmem_limit_bytes=16 << 20),
        cost_estimate=pl.CostEstimate(flops=flops, bytes_accessed=moved, transcendentals=0),
    )(*args)


def swaps():
    tall, broad = lax.axis_size("narrow"), lax.axis_size("wide")
    found = []
    for m in (0, 1):
        pairs = []
        for w in range(broad):
            for i in range(m, tall - 1, 2):
                pairs.append(((i, w), (i + 1, w)))
        if m == 1 and tall <= 4:
            pairs += [((0, w), (tall - 1, w)) for w in range(broad)]
        elif m == 1:
            pairs += [((i, w), (i, w + 1)) for i in (0, tall - 1) for w in range(0, broad, 2)]
        found.append(pairs)
    for m in (0, 1):
        pairs = []
        for i in range(tall):
            for w in range(m, broad - 1, 2):
                pairs.append(((i, w), (i, w + 1)))
        if m == 1:
            pairs += [((i, w), (i + 1, w)) for w in (0, broad - 1) for i in range(0, tall, 2)]
        found.append(pairs)
    flat = []
    for pairs in found:
        ends = [(a[0] * broad + a[1], b[0] * broad + b[1]) for a, b in pairs]
        flat.append([p for a, b in ends for p in ((a, b), (b, a))])
    return flat


def exchange(payloads, half):
    pairs = swaps()
    order = ORDER[2 * half : 2 * half + 2]
    return [lax.ppermute(payload, ("narrow", "wide"), pairs[m]) for payload, m in zip(payloads, order)]


def body(start_block, weights, pattern):
    x = start_block[0, 0]
    w = weights[0, 0]
    slots_of = jnp.transpose(pattern, (0, 3, 1, 2))[0]
    shape = (lax.axis_size("narrow"), lax.axis_size("wide"))
    vecs, docs = x.shape
    blocks, slots = w.shape[:2]
    rows = RIMS * RIM
    tile = ((blocks, vecs, LANES), F32)
    full = ((vecs, docs), F32)
    payload = [((2 * RIM, vecs, LANES), BF16)] * 2
    per_block = 2 * LANES * LANES

    *pays, slots_of = kernel_call(
        functools.partial(outgoing_ones, shape), "outgoing_ones", [("hbm", slots_of), ("hbm", w)],
        [((8, LANES), F32)] * 4 + [(slots_of.shape, jnp.int32)],
        [pltpu.VMEM((rows, slots - INNER, LANES, LANES), BF16), pltpu.SemaphoreType.DMA((PARTS + 1,))]
        + [pltpu.VMEM((RIM, 8, LANES), F32)] * RIMS,
        flops=rows * 3 * per_block * 32, moved=1 << 20,
    )
    w, *pays = lax.optimization_barrier((w, *pays))
    names = [("smem", slots_of)]
    held = names + [("held", w)]
    (degree,) = kernel_call(
        functools.partial(local_degree, shape), "local_degree", held, [((blocks, LANES), F32)],
        [pltpu.VMEM((blocks, 8, LANES), F32)] * 4,
        flops=blocks * slots * per_block * 32, moved=8 << 20,
    )
    got = [exchange(pays[:2], 0), exchange(pays[2:], 1)]
    ext = pltpu.VMEM((4 * RIM, vecs, LANES), BF16)
    terms = pltpu.VMEM((2 * RIM, vecs, LANES), F32)
    count = [len(half) for half in halves(blocks)]
    inv, u, pays = [None] * 2, [None] * 2, [None] * 2
    for half in (0, 1):
        inv[half], u[half], *pays[half] = kernel_call(
            functools.partial(first_scaled, shape, half), "first_scaled",
            held + [("vmem", degree), ("vmem", x)] + [("vmem", g) for g in got[half]],
            [((count[half], LANES), F32), ((count[half], vecs, LANES), BF16)] + payload,
            [pltpu.VMEM((2, 8, LANES), F32), terms],
            flops=rows * 3 * per_block * 16, moved=1 << 19,
        )
    before, y = [x, x], [x, x]
    for step in range(3):
        cost = dict(flops=2 * blocks * slots * per_block * vecs, moved=8 << 20)
        u_ins = [("vmem", part) for part in u]
        u_whole = [pltpu.VMEM((blocks, vecs, LANES), BF16)]
        if step == 0:
            acc, turned = kernel_call(
                own_terms_turning, "own_terms_turning", held + u_ins, [tile, (w.shape, BF16)], u_whole, **cost
            )
        else:
            (acc,) = kernel_call(own_terms, "own_terms", held + [("held", turned)] + u_ins, [tile], u_whole, **cost)
        got = [exchange(pays[0], 0), exchange(pays[1], 1)]
        ins = [
            [("vmem", inv[half])] + [("vmem", g) for g in got[half]] + [("vmem", y[half]), ("vmem", before[half])]
            for half in (0, 1)
        ]
        if step < 2:
            new, u, pays = [None] * 2, [None] * 2, [None] * 2
            for half in (0, 1):
                new[half], u[half], *pays[half] = kernel_call(
                    functools.partial(advance, shape, step, half), "advance",
                    held + [("held", turned), ins[half][0], ("vmem", acc)] + ins[half][1:],
                    [((vecs, count[half] * LANES), F32), ((count[half], vecs, LANES), BF16)] + payload,
                    [ext, terms],
                    flops=rows * 3 * per_block * 32, moved=1 << 19,
                )
            before, y = y, new
        else:
            peers = shape[0] * shape[1]
            packed = ((8, LANES), F32)
            new, more = [None] * 2, []
            for half in (0, 1):
                new[half], grams = kernel_call(
                    functools.partial(finish, shape, half), "finish",
                    names + [("held", turned), ins[half][0], ("vmem", acc)] + ins[half][1:] + more,
                    [((vecs, count[half] * LANES), F32), packed if half == 0 else ((peers, 8, LANES), F32)], [ext],
                    flops=rows * 3 * per_block * 16, moved=1 << 19,
                )
                more = [("vmem", grams)]
            y = new
    grams = lax.all_to_all(grams, ("narrow", "wide"), 0, 0)
    (out,) = kernel_call(
        functools.partial(orthonormal, math.sqrt(peers * docs)), "orthonormal",
        [("vmem", grams), ("vmem", y[0]), ("vmem", y[1])], [full],
    )
    return out[None, None]


def solution(mesh):
    placed = (
        P("narrow", "wide", None, None),
        P("narrow", "wide", None, None, None, None),
        P("narrow", "wide", None, None),
    )
    return jax.shard_map(
        body, mesh=mesh, in_specs=placed, out_specs=P("narrow", "wide", None, None), check_vma=False
    )
```

```python
import functools
import math

import jax
import jax.numpy as jnp
from jax import lax
from jax.experimental import pallas as pl
from jax.experimental.pallas import tpu as pltpu
from jax.sharding import PartitionSpec as P

RIM = 6
RIMS = 4
INNER = 9
PARTS = 3
LANES = 128
F32 = jnp.float32
BF16 = jnp.bfloat16

lower_edge = 0.3
center = (2.0 + lower_edge) / 2.0
half_width = (2.0 - lower_edge) / 2.0

ROWS_BY_ROWS = (((1,), (1,)), ((), ()))
ROWS_BY_COLS = (((1,), (0,)), ((), ()))


def mm(left, right, dims):
    return lax.dot_general(left, right, dims, preferred_element_type=F32)


def three(x):
    high = x.astype(BF16)
    rest = x - high.astype(F32)
    mid = rest.astype(BF16)
    return high, mid, (rest - mid.astype(F32)).astype(BF16)


def beside(parts):
    return parts[0] if len(parts) == 1 else jnp.concatenate(parts, axis=1)


def over(parts):
    return parts[0] if len(parts) == 1 else jnp.concatenate(parts, axis=0)


def slot_pairs(first, last):
    return [list(range(s, min(s + 2, last))) for s in range(first, last, 2)]


def column(b):
    return pl.ds(b * LANES, LANES)


ORDER = (2, 3, 1, 0)


def places(shape):
    rim_of, live_of, by_rim = [], [], []
    for a, axis in enumerate(("narrow", "wide")):
        place = lax.axis_index(axis)
        behind = (place > 0).astype(jnp.int32)
        ahead = (place < shape[a] - 1).astype(jnp.int32)
        odd = lax.rem(place, 2)
        for m in (0, 1):
            after = odd if m else 1 - odd
            rim_of.append(2 * a + after)
            live_of.append(after * ahead + (1 - after) * behind)
        by_rim += [behind, ahead]
    return [rim_of[m] for m in ORDER], [live_of[m] for m in ORDER], by_rim


def fetch(source, target, sem):
    copy = pltpu.make_async_copy(source, target, sem)
    copy.start()
    return copy


def outgoing_ones(shape, pattern_hbm, w_hbm, *refs):
    pay_refs, (pattern_ref, w_ref, sems), sums = refs[:4], refs[4:7], refs[7:]
    named = fetch(pattern_hbm, pattern_ref, sems.at[PARTS])
    copies = []
    for part in range(PARTS):
        rows = pl.ds(part * RIMS * RIM // PARTS, RIMS * RIM // PARTS)
        copies.append(fetch(w_hbm.at[rows, INNER:], w_ref.at[rows], sems.at[part]))
    blocks = pattern_ref.shape[2]
    slots = w_ref.shape[1]
    for r in range(RIMS):
        sums[r][...] = jnp.zeros_like(sums[r])
    ones = jnp.ones((8, LANES), BF16)
    named.wait()
    for p in range(PARTS):
        copies[p].wait()
        for b in range(p * RIMS * RIM // PARTS, (p + 1) * RIMS * RIM // PARTS):
            part = mm(ones, beside([w_ref[b, s] for s in range(slots)]), ROWS_BY_COLS)
            for s in range(slots):
                sums[b // RIM][pattern_ref[INNER + s, 0, b] - blocks] += part[:, s * LANES : (s + 1) * LANES]
    rim_of, _, _ = places(shape)
    for m in range(4):
        low = ORDER[m] // 2 * 2
        upper = (rim_of[m] - low).astype(F32)
        for q in range(RIM):
            total = sums[low][q, 0:1] * (1.0 - upper) + sums[low + 1][q, 0:1] * upper
            pay_refs[m][q : q + 1] = total.astype(BF16).astype(F32)


def local_degree(shape, pattern_ref, w_ref, deg_ref, *accs):
    blocks, slots = w_ref.shape[:2]
    by_rim = places(shape)[2]
    ones = jnp.ones((8, LANES), BF16)
    for b in range(0, blocks, 2):
        part = mm(ones, beside([w_ref[b, 0], w_ref[b + 1, 0]]), ROWS_BY_COLS)
        accs[0][b] = part[:, :LANES]
        accs[0][b + 1] = part[:, LANES:]
    for acc in accs[1:]:
        acc[...] = jnp.zeros_like(acc)
    for b in range(blocks):
        own = INNER if b < RIMS * RIM else slots
        for group in slot_pairs(1, own):
            part = mm(ones, beside([w_ref[b, s] for s in group]), ROWS_BY_COLS)
            for i, s in enumerate(group):
                accs[s % len(accs)][pattern_ref[s, 0, b]] += part[:, i * LANES : (i + 1) * LANES]
        rows = w_ref[b, 0].astype(F32)
        for s in range(1, own):
            rows = rows + w_ref[b, s].astype(F32)
        if own < slots:
            outer = w_ref[b, own].astype(F32)
            for s in range(own + 1, slots):
                outer = outer + w_ref[b, s].astype(F32)
            rows = rows + by_rim[b // RIM].astype(F32) * outer
        deg_ref[b : b + 1] = jnp.sum(rows, axis=1, keepdims=True).T
    for b in range(blocks):
        deg_ref[b : b + 1] += sum(acc[b, 0:1] for acc in accs)


def halves(blocks):
    wide = tuple(range(2 * RIM, RIMS * RIM))
    return wide, tuple(b for b in range(blocks) if b not in wide)


def first_rim(half):
    return 2 - 2 * half


def send_out(shape, half, u_ref, w_ref, pattern_ref, terms, pay_refs):
    blocks, slots = w_ref.shape[:2]
    terms[...] = jnp.zeros_like(terms)
    for i in range(2 * RIM):
        b = first_rim(half) * RIM + i
        part = mm(u_ref[i], beside([w_ref[b, s] for s in range(INNER, slots)]), ROWS_BY_COLS)
        base = i // RIM * RIM - blocks
        for s in range(INNER, slots):
            at = s - INNER
            terms[base + pattern_ref[s, 0, b]] += part[:, at * LANES : (at + 1) * LANES]
    rim_of, _, _ = places(shape)
    for k in range(2):
        first = (rim_of[2 * half + k] - first_rim(half)) * RIM
        pay_refs[k][0:RIM] = u_ref[pl.ds(first, RIM)]
        pay_refs[k][RIM:] = terms[pl.ds(first, RIM)].astype(BF16)


def first_scaled(shape, half, pattern_ref, w_ref, deg_ref, x_ref, *refs):
    in_refs, (inv_ref, u_ref), pay_refs, (rims, terms) = refs[:2], refs[2:4], refs[4:6], refs[6:]
    rim_of, live_of, _ = places(shape)
    for k in range(2):
        m = 2 * half + k
        rims[rim_of[m] - first_rim(half)] = in_refs[k][...] * live_of[m].astype(F32)
    for i, b in enumerate(halves(w_ref.shape[0])[half]):
        degree = deg_ref[b : b + 1]
        if b < RIMS * RIM:
            degree = degree + rims[i // RIM, b % RIM : b % RIM + 1]
        inv = 1.0 / jnp.sqrt(0.5 * degree)
        inv_ref[i : i + 1] = inv
        u_ref[i] = (inv * x_ref[:, column(b)].astype(F32)).astype(BF16)
    send_out(shape, half, u_ref, w_ref, pattern_ref, terms, pay_refs)


def gather_halves(u_refs, u):
    for part_ref, blocks in zip(u_refs, halves(u.shape[0])):
        for i, b in enumerate(blocks):
            u[b] = part_ref[i]


def own_products(pattern_ref, w_ref, turned, u_ref, acc_ref):
    blocks, slots = w_ref.shape[:2]
    for b in range(blocks):
        acc_ref[b] = mm(u_ref[b], turned(b, 0), ROWS_BY_COLS)
    for b in range(blocks):
        group = range(1, INNER if b < RIMS * RIM else slots)
        part = mm(u_ref[b], beside([w_ref[b, s] for s in group]), ROWS_BY_COLS)
        for i, s in enumerate(group):
            acc_ref[pattern_ref[s, 0, b]] += part[:, i * LANES : (i + 1) * LANES]
        ahead = beside([u_ref[pattern_ref[s, 0, b]] for s in group])
        acc_ref[b] += mm(ahead, over([turned(b, s) for s in group]), ROWS_BY_COLS)


def own_terms(pattern_ref, w_ref, turned_ref, u_wide, u_rest, acc_ref, u):
    gather_halves((u_wide, u_rest), u)
    own_products(pattern_ref, w_ref, lambda b, s: turned_ref[b, s], u, acc_ref)


def own_terms_turning(pattern_ref, w_ref, u_wide, u_rest, acc_ref, turned_ref, u):
    blocks, slots = w_ref.shape[:2]

    def turned(b, s):
        block = w_ref[b, s].T
        if s == 0:
            block = (block.astype(F32) + w_ref[b, s].astype(F32)).astype(BF16)
        turned_ref[b, s] = block
        return block

    gather_halves((u_wide, u_rest), u)
    own_products(pattern_ref, w_ref, turned, u, acc_ref)
    for b in range(RIMS * RIM):
        for s in range(INNER, slots):
            turned(b, s)


def combine(shape, step, half, pattern_ref, turned_ref, inv_ref, acc_ref, in_refs, y_ref, before_ref, ext, write):
    blocks, slots = turned_ref.shape[:2]
    rim_of, live_of, _ = places(shape)
    for k in range(2):
        m = 2 * half + k
        first = (rim_of[m] - first_rim(half)) * 2 * RIM
        ext[pl.ds(first, 2 * RIM)] = in_refs[k][...] * live_of[m].astype(BF16)
    mine = halves(blocks)[half]

    def vectors(ref, b, i):
        whole = ref.shape[1] == blocks * LANES
        return ref[:, column(b if whole else i)].astype(F32)

    def update(b, i, total):
        inv = inv_ref[i : i + 1]
        y = vectors(y_ref, b, i)
        lap = y - inv * (0.5 * total)
        new = (lap - center * y) / half_width
        if step > 0:
            new = 2.0 * new - vectors(before_ref, b, i)
        write(b, i, new, inv)

    for i in range(2 * RIM, len(mine)):
        update(mine[i], i, acc_ref[mine[i]])
    for i in range(2 * RIM):
        b = mine[i]
        base = i // RIM * 2 * RIM
        ahead = beside([ext[base + pattern_ref[s, 0, b] - blocks] for s in range(INNER, slots)])
        ahead = mm(ahead, over([turned_ref[b, s] for s in range(INNER, slots)]), ROWS_BY_COLS)
        update(b, i, acc_ref[b] + ahead + ext[base + RIM + b % RIM].astype(F32))


def advance(shape, step, half, pattern_ref, w_ref, turned_ref, inv_ref, acc_ref, *refs):
    in_refs, (y_ref, before_ref, next_ref, u_ref), pay_refs, (ext, terms) = refs[:2], refs[2:6], refs[6:8], refs[8:]

    def write(b, i, new, inv):
        next_ref[:, column(i)] = new
        u_ref[i] = (inv * new).astype(BF16)

    combine(
        shape, step, half, pattern_ref, turned_ref, inv_ref, acc_ref, in_refs, y_ref, before_ref, ext, write
    )
    send_out(shape, half, u_ref, w_ref, pattern_ref, terms, pay_refs)


def finish(shape, half, pattern_ref, turned_ref, inv_ref, acc_ref, *refs):
    in_refs, (y_ref, before_ref), refs = refs[:2], refs[2:4], refs[4:]
    next_ref, gram_ref, ext = refs[-3:]

    def write(b, i, new, inv):
        next_ref[:, column(i)] = new

    combine(shape, 2, half, pattern_ref, turned_ref, inv_ref, acc_ref, in_refs, y_ref, before_ref, ext, write)
    n = next_ref.shape[0]
    terms = over(three(next_ref[...]))
    every = mm(terms, terms, ROWS_BY_ROWS)
    gram = sum(every[n * i : n * (i + 1), n * j : n * (j + 1)] for i, j in ((0, 2), (2, 0), (1, 1), (0, 1), (1, 0), (0, 0)))
    packed = beside([gram[8 * i : 8 * i + 8] for i in range(n // 8)])
    if half == 0:
        gram_ref[...] = packed
    else:
        gram_ref[...] = jnp.broadcast_to((packed + refs[0][...])[None], gram_ref.shape)


def inverse_factor(gram, scale):
    n = gram.shape[0]
    tall = 8
    groups = range(n // tall)
    lane = lax.broadcasted_iota(jnp.int32, (tall, LANES), 1)
    sub = lax.broadcasted_iota(jnp.int32, (tall, LANES), 0)

    def spread(values, r):
        return jnp.broadcast_to(values[r : r + 1], (tall, LANES))

    both = []
    for i in groups:
        eye = (lane[:, :n] == sub[:, :n] + tall * i).astype(F32)
        both.append(beside([gram[tall * i : tall * (i + 1)], eye, jnp.zeros((tall, LANES - 2 * n), F32)]))
    parts = []
    for q in groups:
        columns = [
            {i: jnp.broadcast_to(both[i][:, tall * q + j : tall * q + j + 1], (tall, LANES)) for i in groups if i >= q}
            for j in range(tall)
        ]
        pivots = None
        for r in range(tall):
            pivot = spread(columns[r][q], r)
            pivots = pivot if pivots is None else jnp.where(sub == r, pivot, pivots)
            inv = 1.0 / pivot
            row = spread(both[q], r) * inv
            below = dict(columns[r])
            below[q] = jnp.where(sub > r, below[q], 0.0)
            live = [i for i in groups if i > q or (i == q and r < tall - 1)]
            for j in range(r + 1, tall):
                scaled = spread(columns[j][q], r) * inv
                for i in live:
                    columns[j][i] = columns[j][i] - below[i] * scaled
            for i in live:
                both[i] = both[i] - below[i] * row
        parts.append((both[q] * (scale / jnp.sqrt(pivots)))[:, n : 2 * n])
    return over(parts)


def orthonormal(scale, grams_ref, wide_ref, rest_ref, out_ref):
    packed = jnp.sum(grams_ref[...], axis=0)
    n = wide_ref.shape[0]
    gram = over([packed[:, n * i : n * (i + 1)] for i in range(n // 8)])
    a = three(inverse_factor(gram, scale))
    pairs = ((0, 0), (0, 1), (1, 0), (0, 2), (1, 1), (2, 0))
    left = beside([a[i] for i, _ in pairs])
    width = 4 * LANES
    at = 0
    for ref, first in ((rest_ref, 0), (wide_ref, 0), (rest_ref, 2 * RIM * LANES)):
        last = 2 * RIM * LANES if first == 0 else ref.shape[1]
        for start in range(first, last, width):
            y = three(ref[:, start : start + width])
            out_ref[:, at : at + width] = mm(left, over([y[j] for _, j in pairs]), ROWS_BY_COLS)
            at += width


def in_vmem(x):
    return pltpu.with_memory_space_constraint(x, pltpu.VMEM)


def kernel_call(body, name, ins, outs, scratch=(), flops=0, moved=0):
    specs, args = [], []
    for kind, x in ins:
        if kind == "hbm":
            specs.append(pl.BlockSpec(memory_space=pl.ANY))
            x = pltpu.with_memory_space_constraint(x, pltpu.HBM)
        elif kind == "smem":
            specs.append(pl.BlockSpec(memory_space=pltpu.SMEM))
            x = pltpu.with_memory_space_constraint(x, pltpu.SMEM)
        else:
            specs.append(pl.BlockSpec(memory_space=pltpu.VMEM))
            if kind == "held":
                x = in_vmem(x)
        args.append(x)
    return pl.pallas_call(
        body,
        name=name,
        out_shape=[
            pltpu.SMEM(s, d) if d == jnp.int32 else pltpu.VMEM(s, d) if len(s) == 4 else jax.ShapeDtypeStruct(s, d)
            for s, d in outs
        ],
        in_specs=specs,
        out_specs=[pl.BlockSpec(memory_space=pltpu.SMEM if d == jnp.int32 else pltpu.VMEM) for _, d in outs],
        scratch_shapes=list(scratch),
        compiler_params=pltpu.CompilerParams(vmem_limit_bytes=16 << 20),
        cost_estimate=pl.CostEstimate(flops=flops, bytes_accessed=moved, transcendentals=0),
    )(*args)


def swaps():
    tall, broad = lax.axis_size("narrow"), lax.axis_size("wide")
    found = []
    for m in (0, 1):
        pairs = []
        for w in range(broad):
            for i in range(m, tall - 1, 2):
                pairs.append(((i, w), (i + 1, w)))
        if m == 1 and tall <= 4:
            pairs += [((0, w), (tall - 1, w)) for w in range(broad)]
        elif m == 1:
            pairs += [((i, w), (i, w + 1)) for i in (0, tall - 1) for w in range(0, broad, 2)]
        found.append(pairs)
    for m in (0, 1):
        pairs = []
        for i in range(tall):
            for w in range(m, broad - 1, 2):
                pairs.append(((i, w), (i, w + 1)))
        if m == 1:
            pairs += [((i, w), (i + 1, w)) for w in (0, broad - 1) for i in range(0, tall, 2)]
        found.append(pairs)
    flat = []
    for pairs in found:
        ends = [(a[0] * broad + a[1], b[0] * broad + b[1]) for a, b in pairs]
        flat.append([p for a, b in ends for p in ((a, b), (b, a))])
    return flat


def exchange(payloads, half):
    pairs = swaps()
    order = ORDER[2 * half : 2 * half + 2]
    return [lax.ppermute(payload, ("narrow", "wide"), pairs[m]) for payload, m in zip(payloads, order)]


def body(start_block, weights, pattern):
    x = start_block[0, 0]
    w = weights[0, 0]
    slots_of = jnp.transpose(pattern, (0, 3, 1, 2))[0]
    shape = (lax.axis_size("narrow"), lax.axis_size("wide"))
    vecs, docs = x.shape
    blocks, slots = w.shape[:2]
    rows = RIMS * RIM
    tile = ((blocks, vecs, LANES), F32)
    full = ((vecs, docs), F32)
    payload = [((2 * RIM, vecs, LANES), BF16)] * 2
    per_block = 2 * LANES * LANES

    *pays, slots_of = kernel_call(
        functools.partial(outgoing_ones, shape), "outgoing_ones", [("hbm", slots_of), ("hbm", w)],
        [((8, LANES), F32)] * 4 + [(slots_of.shape, jnp.int32)],
        [pltpu.VMEM((rows, slots - INNER, LANES, LANES), BF16), pltpu.SemaphoreType.DMA((PARTS + 1,))]
        + [pltpu.VMEM((RIM, 8, LANES), F32)] * RIMS,
        flops=rows * 3 * per_block * 32, moved=1 << 20,
    )
    w, *pays = lax.optimization_barrier((w, *pays))
    names = [("smem", slots_of)]
    held = names + [("held", w)]
    (degree,) = kernel_call(
        functools.partial(local_degree, shape), "local_degree", held, [((blocks, LANES), F32)],
        [pltpu.VMEM((blocks, 8, LANES), F32)] * 4,
        flops=blocks * slots * per_block * 32, moved=8 << 20,
    )
    got = [exchange(pays[:2], 0), exchange(pays[2:], 1)]
    ext = pltpu.VMEM((4 * RIM, vecs, LANES), BF16)
    terms = pltpu.VMEM((2 * RIM, vecs, LANES), F32)
    count = [len(half) for half in halves(blocks)]
    inv, u, pays = [None] * 2, [None] * 2, [None] * 2
    for half in (0, 1):
        inv[half], u[half], *pays[half] = kernel_call(
            functools.partial(first_scaled, shape, half), "first_scaled",
            held + [("vmem", degree), ("vmem", x)] + [("vmem", g) for g in got[half]],
            [((count[half], LANES), F32), ((count[half], vecs, LANES), BF16)] + payload,
            [pltpu.VMEM((2, 8, LANES), F32), terms],
            flops=rows * 3 * per_block * 16, moved=1 << 19,
        )
    before, y = [x, x], [x, x]
    for step in range(3):
        cost = dict(flops=2 * blocks * slots * per_block * vecs, moved=8 << 20)
        u_ins = [("vmem", part) for part in u]
        u_whole = [pltpu.VMEM((blocks, vecs, LANES), BF16)]
        if step == 0:
            acc, turned = kernel_call(
                own_terms_turning, "own_terms_turning", held + u_ins, [tile, (w.shape, BF16)], u_whole, **cost
            )
        else:
            (acc,) = kernel_call(own_terms, "own_terms", held + [("held", turned)] + u_ins, [tile], u_whole, **cost)
        got = [exchange(pays[0], 0), exchange(pays[1], 1)]
        ins = [
            [("vmem", inv[half])] + [("vmem", g) for g in got[half]] + [("vmem", y[half]), ("vmem", before[half])]
            for half in (0, 1)
        ]
        if step < 2:
            new, u, pays = [None] * 2, [None] * 2, [None] * 2
            for half in (0, 1):
                new[half], u[half], *pays[half] = kernel_call(
                    functools.partial(advance, shape, step, half), "advance",
                    held + [("held", turned), ins[half][0], ("vmem", acc)] + ins[half][1:],
                    [((vecs, count[half] * LANES), F32), ((count[half], vecs, LANES), BF16)] + payload,
                    [ext, terms],
                    flops=rows * 3 * per_block * 32, moved=1 << 19,
                )
            before, y = y, new
        else:
            peers = shape[0] * shape[1]
            packed = ((8, LANES), F32)
            new, more = [None] * 2, []
            for half in (0, 1):
                new[half], grams = kernel_call(
                    functools.partial(finish, shape, half), "finish",
                    names + [("held", turned), ins[half][0], ("vmem", acc)] + ins[half][1:] + more,
                    [((vecs, count[half] * LANES), F32), packed if half == 0 else ((peers, 8, LANES), F32)], [ext],
                    flops=rows * 3 * per_block * 16, moved=1 << 19,
                )
                more = [("vmem", grams)]
            y = new
    grams = lax.all_to_all(grams, ("narrow", "wide"), 0, 0)
    (out,) = kernel_call(
        functools.partial(orthonormal, math.sqrt(peers * docs)), "orthonormal",
        [("vmem", grams), ("vmem", y[0]), ("vmem", y[1])], [full],
    )
    return out[None, None]


def solution(mesh):
    placed = (
        P("narrow", "wide", None, None),
        P("narrow", "wide", None, None, None, None),
        P("narrow", "wide", None, None),
    )
    return jax.shard_map(
        body, mesh=mesh, in_specs=placed, out_specs=P("narrow", "wide", None, None), check_vma=False
    )
```

```python
import functools
import math

import jax
import jax.numpy as jnp
from jax import lax
from jax.experimental import pallas as pl
from jax.experimental.pallas import tpu as pltpu
from jax.sharding import PartitionSpec as P

RIM = 6
RIMS = 4
INNER = 9
PARTS = 3
LANES = 128
F32 = jnp.float32
BF16 = jnp.bfloat16

lower_edge = 0.3
center = (2.0 + lower_edge) / 2.0
half_width = (2.0 - lower_edge) / 2.0

ROWS_BY_ROWS = (((1,), (1,)), ((), ()))
ROWS_BY_COLS = (((1,), (0,)), ((), ()))


def mm(left, right, dims):
    return lax.dot_general(left, right, dims, preferred_element_type=F32)


def three(x):
    high = x.astype(BF16)
    rest = x - high.astype(F32)
    mid = rest.astype(BF16)
    return high, mid, (rest - mid.astype(F32)).astype(BF16)


def beside(parts):
    return parts[0] if len(parts) == 1 else jnp.concatenate(parts, axis=1)


def over(parts):
    return parts[0] if len(parts) == 1 else jnp.concatenate(parts, axis=0)


def slot_pairs(first, last):
    return [list(range(s, min(s + 2, last))) for s in range(first, last, 2)]


def column(b):
    return pl.ds(b * LANES, LANES)


ORDER = (2, 3, 1, 0)


def places(shape):
    rim_of, live_of, by_rim = [], [], []
    for a, axis in enumerate(("narrow", "wide")):
        place = lax.axis_index(axis)
        behind = (place > 0).astype(jnp.int32)
        ahead = (place < shape[a] - 1).astype(jnp.int32)
        odd = lax.rem(place, 2)
        for m in (0, 1):
            after = odd if m else 1 - odd
            rim_of.append(2 * a + after)
            live_of.append(after * ahead + (1 - after) * behind)
        by_rim += [behind, ahead]
    return [rim_of[m] for m in ORDER], [live_of[m] for m in ORDER], by_rim


def fetch(source, target, sem):
    copy = pltpu.make_async_copy(source, target, sem)
    copy.start()
    return copy


def outgoing_ones(shape, pattern_hbm, w_hbm, *refs):
    pay_refs, (pattern_ref, w_ref, sems), sums = refs[:4], refs[4:7], refs[7:]
    named = fetch(pattern_hbm, pattern_ref, sems.at[PARTS])
    copies = []
    for part in range(PARTS):
        rows = pl.ds(part * RIMS * RIM // PARTS, RIMS * RIM // PARTS)
        copies.append(fetch(w_hbm.at[rows, INNER:], w_ref.at[rows], sems.at[part]))
    blocks = pattern_ref.shape[2]
    slots = w_ref.shape[1]
    for r in range(RIMS):
        sums[r][...] = jnp.zeros_like(sums[r])
    ones = jnp.ones((8, LANES), BF16)
    named.wait()
    for p in range(PARTS):
        copies[p].wait()
        for b in range(p * RIMS * RIM // PARTS, (p + 1) * RIMS * RIM // PARTS):
            part = mm(ones, beside([w_ref[b, s] for s in range(slots)]), ROWS_BY_COLS)
            for s in range(slots):
                sums[b // RIM][pattern_ref[INNER + s, 0, b] - blocks] += part[:, s * LANES : (s + 1) * LANES]
    rim_of, _, _ = places(shape)
    for m in range(4):
        low = ORDER[m] // 2 * 2
        upper = (rim_of[m] - low).astype(F32)
        for q in range(RIM):
            total = sums[low][q, 0:1] * (1.0 - upper) + sums[low + 1][q, 0:1] * upper
            pay_refs[m][q : q + 1] = total.astype(BF16).astype(F32)


def local_degree(shape, pattern_ref, w_ref, deg_ref, *accs):
    blocks, slots = w_ref.shape[:2]
    by_rim = places(shape)[2]
    ones = jnp.ones((8, LANES), BF16)
    for b in range(0, blocks, 2):
        part = mm(ones, beside([w_ref[b, 0], w_ref[b + 1, 0]]), ROWS_BY_COLS)
        accs[0][b] = part[:, :LANES]
        accs[0][b + 1] = part[:, LANES:]
    for acc in accs[1:]:
        acc[...] = jnp.zeros_like(acc)
    for b in range(blocks):
        own = INNER if b < RIMS * RIM else slots
        for group in slot_pairs(1, own):
            part = mm(ones, beside([w_ref[b, s] for s in group]), ROWS_BY_COLS)
            for i, s in enumerate(group):
                accs[s % len(accs)][pattern_ref[s, 0, b]] += part[:, i * LANES : (i + 1) * LANES]
        rows = w_ref[b, 0].astype(F32)
        for s in range(1, own):
            rows = rows + w_ref[b, s].astype(F32)
        if own < slots:
            outer = w_ref[b, own].astype(F32)
            for s in range(own + 1, slots):
                outer = outer + w_ref[b, s].astype(F32)
            rows = rows + by_rim[b // RIM].astype(F32) * outer
        deg_ref[b : b + 1] = jnp.sum(rows, axis=1, keepdims=True).T
    for b in range(blocks):
        deg_ref[b : b + 1] += sum(acc[b, 0:1] for acc in accs)


def halves(blocks):
    wide = tuple(range(2 * RIM, RIMS * RIM))
    return wide, tuple(b for b in range(blocks) if b not in wide)


def first_rim(half):
    return 2 - 2 * half


def send_out(shape, half, u_ref, w_ref, pattern_ref, terms, pay_refs):
    blocks, slots = w_ref.shape[:2]
    terms[...] = jnp.zeros_like(terms)
    for i in range(2 * RIM):
        b = first_rim(half) * RIM + i
        part = mm(u_ref[i], beside([w_ref[b, s] for s in range(INNER, slots)]), ROWS_BY_COLS)
        base = i // RIM * RIM - blocks
        for s in range(INNER, slots):
            at = s - INNER
            terms[base + pattern_ref[s, 0, b]] += part[:, at * LANES : (at + 1) * LANES]
    rim_of, _, _ = places(shape)
    for k in range(2):
        first = (rim_of[2 * half + k] - first_rim(half)) * RIM
        pay_refs[k][0:RIM] = u_ref[pl.ds(first, RIM)]
        pay_refs[k][RIM:] = terms[pl.ds(first, RIM)].astype(BF16)


def first_scaled(shape, half, pattern_ref, w_ref, deg_ref, x_ref, *refs):
    in_refs, (inv_ref, u_ref), pay_refs, (rims, terms) = refs[:2], refs[2:4], refs[4:6], refs[6:]
    rim_of, live_of, _ = places(shape)
    for k in range(2):
        m = 2 * half + k
        rims[rim_of[m] - first_rim(half)] = in_refs[k][...] * live_of[m].astype(F32)
    for i, b in enumerate(halves(w_ref.shape[0])[half]):
        degree = deg_ref[b : b + 1]
        if b < RIMS * RIM:
            degree = degree + rims[i // RIM, b % RIM : b % RIM + 1]
        inv = 1.0 / jnp.sqrt(0.5 * degree)
        inv_ref[i : i + 1] = inv
        u_ref[i] = (inv * x_ref[:, column(b)].astype(F32)).astype(BF16)
    send_out(shape, half, u_ref, w_ref, pattern_ref, terms, pay_refs)


def gather_halves(u_refs, u):
    for part_ref, blocks in zip(u_refs, halves(u.shape[0])):
        for i, b in enumerate(blocks):
            u[b] = part_ref[i]


def own_products(pattern_ref, w_ref, turned, u_ref, acc_ref):
    blocks, slots = w_ref.shape[:2]
    for b in range(blocks):
        acc_ref[b] = mm(u_ref[b], turned(b, 0), ROWS_BY_COLS)
    for b in range(blocks):
        group = range(1, INNER if b < RIMS * RIM else slots)
        part = mm(u_ref[b], beside([w_ref[b, s] for s in group]), ROWS_BY_COLS)
        for i, s in enumerate(group):
            acc_ref[pattern_ref[s, 0, b]] += part[:, i * LANES : (i + 1) * LANES]
        ahead = beside([u_ref[pattern_ref[s, 0, b]] for s in group])
        acc_ref[b] += mm(ahead, over([turned(b, s) for s in group]), ROWS_BY_COLS)


def own_terms(pattern_ref, w_ref, turned_ref, u_wide, u_rest, acc_ref, u):
    gather_halves((u_wide, u_rest), u)
    own_products(pattern_ref, w_ref, lambda b, s: turned_ref[b, s], u, acc_ref)


def own_terms_turning(pattern_ref, w_ref, u_wide, u_rest, acc_ref, turned_ref, u):
    blocks, slots = w_ref.shape[:2]

    def turned(b, s):
        block = w_ref[b, s].T
        if s == 0:
            block = (block.astype(F32) + w_ref[b, s].astype(F32)).astype(BF16)
        turned_ref[b, s] = block
        return block

    gather_halves((u_wide, u_rest), u)
    own_products(pattern_ref, w_ref, turned, u, acc_ref)
    for b in range(RIMS * RIM):
        for s in range(INNER, slots):
            turned(b, s)


def combine(shape, step, half, pattern_ref, turned_ref, inv_ref, acc_ref, in_refs, y_ref, before_ref, ext, write):
    blocks, slots = turned_ref.shape[:2]
    rim_of, live_of, _ = places(shape)
    for k in range(2):
        m = 2 * half + k
        first = (rim_of[m] - first_rim(half)) * 2 * RIM
        ext[pl.ds(first, 2 * RIM)] = in_refs[k][...] * live_of[m].astype(BF16)
    mine = halves(blocks)[half]

    def vectors(ref, b, i):
        whole = ref.shape[1] == blocks * LANES
        return ref[:, column(b if whole else i)].astype(F32)

    def update(b, i, total):
        inv = inv_ref[i : i + 1]
        y = vectors(y_ref, b, i)
        lap = y - inv * (0.5 * total)
        new = (lap - center * y) / half_width
        if step > 0:
            new = 2.0 * new - vectors(before_ref, b, i)
        write(b, i, new, inv)

    for i in range(2 * RIM, len(mine)):
        update(mine[i], i, acc_ref[mine[i]])
    for i in range(2 * RIM):
        b = mine[i]
        base = i // RIM * 2 * RIM
        ahead = beside([ext[base + pattern_ref[s, 0, b] - blocks] for s in range(INNER, slots)])
        ahead = mm(ahead, over([turned_ref[b, s] for s in range(INNER, slots)]), ROWS_BY_COLS)
        update(b, i, acc_ref[b] + ahead + ext[base + RIM + b % RIM].astype(F32))


def advance(shape, step, half, pattern_ref, w_ref, turned_ref, inv_ref, acc_ref, *refs):
    in_refs, (y_ref, before_ref, next_ref, u_ref), pay_refs, (ext, terms) = refs[:2], refs[2:6], refs[6:8], refs[8:]

    def write(b, i, new, inv):
        next_ref[:, column(i)] = new
        u_ref[i] = (inv * new).astype(BF16)

    combine(
        shape, step, half, pattern_ref, turned_ref, inv_ref, acc_ref, in_refs, y_ref, before_ref, ext, write
    )
    send_out(shape, half, u_ref, w_ref, pattern_ref, terms, pay_refs)


def finish(shape, half, pattern_ref, turned_ref, inv_ref, acc_ref, *refs):
    in_refs, (y_ref, before_ref), refs = refs[:2], refs[2:4], refs[4:]
    next_ref, gram_ref, ext = refs[-3:]

    def write(b, i, new, inv):
        next_ref[:, column(i)] = new

    combine(shape, 2, half, pattern_ref, turned_ref, inv_ref, acc_ref, in_refs, y_ref, before_ref, ext, write)
    n = next_ref.shape[0]
    terms = over(three(next_ref[...]))
    every = mm(terms, terms, ROWS_BY_ROWS)
    gram = sum(every[n * i : n * (i + 1), n * j : n * (j + 1)] for i, j in ((0, 2), (2, 0), (1, 1), (0, 1), (1, 0), (0, 0)))
    packed = beside([gram[8 * i : 8 * i + 8] for i in range(n // 8)])
    if half == 0:
        gram_ref[...] = packed
    else:
        gram_ref[...] = jnp.broadcast_to((packed + refs[0][...])[None], gram_ref.shape)


def inverse_factor(gram, scale):
    n = gram.shape[0]
    tall = 8
    groups = range(n // tall)
    lane = lax.broadcasted_iota(jnp.int32, (tall, LANES), 1)
    sub = lax.broadcasted_iota(jnp.int32, (tall, LANES), 0)

    def spread(values, r):
        return jnp.broadcast_to(values[r : r + 1], (tall, LANES))

    both = []
    for i in groups:
        eye = (lane[:, :n] == sub[:, :n] + tall * i).astype(F32)
        both.append(beside([gram[tall * i : tall * (i + 1)], eye, jnp.zeros((tall, LANES - 2 * n), F32)]))
    parts = []
    for q in groups:
        columns = [
            {i: jnp.broadcast_to(both[i][:, tall * q + j : tall * q + j + 1], (tall, LANES)) for i in groups if i >= q}
            for j in range(tall)
        ]
        pivots = None
        for r in range(tall):
            pivot = spread(columns[r][q], r)
            pivots = pivot if pivots is None else jnp.where(sub == r, pivot, pivots)
            inv = 1.0 / pivot
            row = spread(both[q], r) * inv
            below = dict(columns[r])
            below[q] = jnp.where(sub > r, below[q], 0.0)
            live = [i for i in groups if i > q or (i == q and r < tall - 1)]
            for j in range(r + 1, tall):
                scaled = spread(columns[j][q], r) * inv
                for i in live:
                    columns[j][i] = columns[j][i] - below[i] * scaled
            for i in live:
                both[i] = both[i] - below[i] * row
        parts.append((both[q] * (scale / jnp.sqrt(pivots)))[:, n : 2 * n])
    return over(parts)


def orthonormal(scale, grams_ref, wide_ref, rest_ref, out_hbm, out_ref, sems):
    packed = jnp.sum(grams_ref[...], axis=0)
    n = wide_ref.shape[0]
    gram = over([packed[:, n * i : n * (i + 1)] for i in range(n // 8)])
    a = three(inverse_factor(gram, scale))
    pairs = ((0, 0), (0, 1), (1, 0), (0, 2), (1, 1), (2, 0))
    left = beside([a[i] for i, _ in pairs])
    width = 4 * LANES
    at = 0
    copies = []
    for ref, first in ((rest_ref, 0), (wide_ref, 0), (rest_ref, 2 * RIM * LANES)):
        last = 2 * RIM * LANES if first == 0 else ref.shape[1]
        for start in range(first, last, width):
            y = three(ref[:, start : start + width])
            out_ref[:, at : at + width] = mm(left, over([y[j] for _, j in pairs]), ROWS_BY_COLS)
            piece = pl.ds(at, width)
            copies.append(fetch(out_ref.at[:, piece], out_hbm.at[:, piece], sems.at[at // width]))
            at += width
    for copy in copies:
        copy.wait()


def in_vmem(x):
    return pltpu.with_memory_space_constraint(x, pltpu.VMEM)


def kernel_call(body, name, ins, outs, scratch=(), flops=0, moved=0, out_at=pltpu.VMEM):
    specs, args = [], []
    for kind, x in ins:
        if kind == "hbm":
            specs.append(pl.BlockSpec(memory_space=pl.ANY))
            x = pltpu.with_memory_space_constraint(x, pltpu.HBM)
        elif kind == "smem":
            specs.append(pl.BlockSpec(memory_space=pltpu.SMEM))
            x = pltpu.with_memory_space_constraint(x, pltpu.SMEM)
        else:
            specs.append(pl.BlockSpec(memory_space=pltpu.VMEM))
            if kind == "held":
                x = in_vmem(x)
        args.append(x)
    return pl.pallas_call(
        body,
        name=name,
        out_shape=[
            pltpu.SMEM(s, d) if d == jnp.int32 else pltpu.VMEM(s, d) if len(s) == 4 else jax.ShapeDtypeStruct(s, d)
            for s, d in outs
        ],
        in_specs=specs,
        out_specs=[pl.BlockSpec(memory_space=pltpu.SMEM if d == jnp.int32 else out_at) for _, d in outs],
        scratch_shapes=list(scratch),
        compiler_params=pltpu.CompilerParams(vmem_limit_bytes=16 << 20),
        cost_estimate=pl.CostEstimate(flops=flops, bytes_accessed=moved, transcendentals=0),
    )(*args)


def swaps():
    tall, broad = lax.axis_size("narrow"), lax.axis_size("wide")
    found = []
    for m in (0, 1):
        pairs = []
        for w in range(broad):
            for i in range(m, tall - 1, 2):
                pairs.append(((i, w), (i + 1, w)))
        if m == 1 and tall <= 4:
            pairs += [((0, w), (tall - 1, w)) for w in range(broad)]
        elif m == 1:
            pairs += [((i, w), (i, w + 1)) for i in (0, tall - 1) for w in range(0, broad, 2)]
        found.append(pairs)
    for m in (0, 1):
        pairs = []
        for i in range(tall):
            for w in range(m, broad - 1, 2):
                pairs.append(((i, w), (i, w + 1)))
        if m == 1:
            pairs += [((i, w), (i + 1, w)) for w in (0, broad - 1) for i in range(0, tall, 2)]
        found.append(pairs)
    flat = []
    for pairs in found:
        ends = [(a[0] * broad + a[1], b[0] * broad + b[1]) for a, b in pairs]
        flat.append([p for a, b in ends for p in ((a, b), (b, a))])
    return flat


def exchange(payloads, half):
    pairs = swaps()
    order = ORDER[2 * half : 2 * half + 2]
    return [lax.ppermute(payload, ("narrow", "wide"), pairs[m]) for payload, m in zip(payloads, order)]


def body(start_block, weights, pattern):
    x = start_block[0, 0]
    w = weights[0, 0]
    slots_of = jnp.transpose(pattern, (0, 3, 1, 2))[0]
    shape = (lax.axis_size("narrow"), lax.axis_size("wide"))
    vecs, docs = x.shape
    blocks, slots = w.shape[:2]
    rows = RIMS * RIM
    tile = ((blocks, vecs, LANES), F32)
    full = ((vecs, docs), F32)
    payload = [((2 * RIM, vecs, LANES), BF16)] * 2
    per_block = 2 * LANES * LANES

    *pays, slots_of = kernel_call(
        functools.partial(outgoing_ones, shape), "outgoing_ones", [("hbm", slots_of), ("hbm", w)],
        [((8, LANES), F32)] * 4 + [(slots_of.shape, jnp.int32)],
        [pltpu.VMEM((rows, slots - INNER, LANES, LANES), BF16), pltpu.SemaphoreType.DMA((PARTS + 1,))]
        + [pltpu.VMEM((RIM, 8, LANES), F32)] * RIMS,
        flops=rows * 3 * per_block * 32, moved=1 << 20,
    )
    w, *pays = lax.optimization_barrier((w, *pays))
    names = [("smem", slots_of)]
    held = names + [("held", w)]
    (degree,) = kernel_call(
        functools.partial(local_degree, shape), "local_degree", held, [((blocks, LANES), F32)],
        [pltpu.VMEM((blocks, 8, LANES), F32)] * 4,
        flops=blocks * slots * per_block * 32, moved=8 << 20,
    )
    got = [exchange(pays[:2], 0), exchange(pays[2:], 1)]
    ext = pltpu.VMEM((4 * RIM, vecs, LANES), BF16)
    terms = pltpu.VMEM((2 * RIM, vecs, LANES), F32)
    count = [len(half) for half in halves(blocks)]
    inv, u, pays = [None] * 2, [None] * 2, [None] * 2
    for half in (0, 1):
        inv[half], u[half], *pays[half] = kernel_call(
            functools.partial(first_scaled, shape, half), "first_scaled",
            held + [("vmem", degree), ("vmem", x)] + [("vmem", g) for g in got[half]],
            [((count[half], LANES), F32), ((count[half], vecs, LANES), BF16)] + payload,
            [pltpu.VMEM((2, 8, LANES), F32), terms],
            flops=rows * 3 * per_block * 16, moved=1 << 19,
        )
    before, y = [x, x], [x, x]
    for step in range(3):
        cost = dict(flops=2 * blocks * slots * per_block * vecs, moved=8 << 20)
        u_ins = [("vmem", part) for part in u]
        u_whole = [pltpu.VMEM((blocks, vecs, LANES), BF16)]
        if step == 0:
            acc, turned = kernel_call(
                own_terms_turning, "own_terms_turning", held + u_ins, [tile, (w.shape, BF16)], u_whole, **cost
            )
        else:
            (acc,) = kernel_call(own_terms, "own_terms", held + [("held", turned)] + u_ins, [tile], u_whole, **cost)
        got = [exchange(pays[0], 0), exchange(pays[1], 1)]
        ins = [
            [("vmem", inv[half])] + [("vmem", g) for g in got[half]] + [("vmem", y[half]), ("vmem", before[half])]
            for half in (0, 1)
        ]
        if step < 2:
            new, u, pays = [None] * 2, [None] * 2, [None] * 2
            for half in (0, 1):
                new[half], u[half], *pays[half] = kernel_call(
                    functools.partial(advance, shape, step, half), "advance",
                    held + [("held", turned), ins[half][0], ("vmem", acc)] + ins[half][1:],
                    [((vecs, count[half] * LANES), F32), ((count[half], vecs, LANES), BF16)] + payload,
                    [ext, terms],
                    flops=rows * 3 * per_block * 32, moved=1 << 19,
                )
            before, y = y, new
        else:
            peers = shape[0] * shape[1]
            packed = ((8, LANES), F32)
            new, more = [None] * 2, []
            for half in (0, 1):
                new[half], grams = kernel_call(
                    functools.partial(finish, shape, half), "finish",
                    names + [("held", turned), ins[half][0], ("vmem", acc)] + ins[half][1:] + more,
                    [((vecs, count[half] * LANES), F32), packed if half == 0 else ((peers, 8, LANES), F32)], [ext],
                    flops=rows * 3 * per_block * 16, moved=1 << 19,
                )
                more = [("vmem", grams)]
            y = new
    grams = lax.all_to_all(grams, ("narrow", "wide"), 0, 0)
    (out,) = kernel_call(
        functools.partial(orthonormal, math.sqrt(peers * docs)), "orthonormal",
        [("vmem", grams), ("vmem", y[0]), ("vmem", y[1])], [full],
        [pltpu.VMEM(*full), pltpu.SemaphoreType.DMA((docs // (4 * LANES),))], out_at=pl.ANY,
    )
    return out[None, None]


def solution(mesh):
    placed = (
        P("narrow", "wide", None, None),
        P("narrow", "wide", None, None, None, None),
        P("narrow", "wide", None, None),
    )
    return jax.shard_map(
        body, mesh=mesh, in_specs=placed, out_specs=P("narrow", "wide", None, None), check_vma=False
    )
```
